32 devices in a mesh: seq: 8 (over z, x), head: 4 (over y, core).
Axes of the slice: x: 2, y: 2, z: 4, core: 2. Of those that a mesh axis runs over, the one named last changes fastest.
Arguments:
- queries: bfloat16 [4096, 8192], P('seq', 'head'), may hold values from -0.5 to 0.5
- keys: bfloat16 [4096, 8192], P('seq', 'head'), may hold values from -6 to 6
- values: bfloat16 [4096, 8192], P('seq', 'head'), may hold values from -6 to 6
- cotangent: bfloat16 [4096, 8192], P('seq', 'head'), may hold values from -6 to 6
- log_decay: float32 [64, 4096], P('head', 'seq'), may hold values from -0.6 to 0
- starts: int32 [4096], P('seq'), may hold values 0 or 1
Outputs:
- attn_out: bfloat16 [4096, 8192], P('seq', 'head')
- grad_query: bfloat16 [4096, 8192], P('seq', 'head')
- grad_key: bfloat16 [4096, 8192], P('seq', 'head')
- grad_value: bfloat16 [4096, 8192], P('seq', 'head')
The draws below stay inside these ranges and needn't reach their ends.
All inputs are finite; a program needn't handle non-finite values. No bound on the sum of `starts` on one device may be relied on, other than what follows from the above.
Results may differ from the reference program's by a relative error of at most 0.0095.
Values may be sent and summed in bfloat16 or wider, within the bound.
No kernel may reach another device: no remote copies, remote signals or barrier semaphores. Data moves between devices by JAX's collectives and lax.ppermute only.
A program may use at most 128 MiB of HBM per device.

```python
import jax
import jax.numpy as jnp
from jax import lax

HEAD_TOTAL = 64
HEAD_DIM = 128
TOK_DEV = 512
WINDOW_TOKENS = 4096


def draw_log_decay(key, part):
    every_key = jax.random.split(key, 7)
    fast_share = 0.5
    fast_head = jax.random.uniform(every_key[0], (HEAD_TOTAL, 1)) < fast_share
    fast_rate = jnp.exp(jax.random.uniform(every_key[1], (HEAD_TOTAL, 1), minval=jnp.log(1.0 / 50.0), maxval=jnp.log(1.0 / 30.0)))
    slow_rate = jax.random.uniform(every_key[2], (HEAD_TOTAL, 1), minval=0.05, maxval=0.4) / WINDOW_TOKENS
    baseline_rate = jnp.where(fast_head, fast_rate, slow_rate)
    block_scaling = jnp.exp(jax.random.uniform(every_key[3], (HEAD_TOTAL, WINDOW_TOKENS // TOK_DEV), minval=-0.4, maxval=0.4))
    block_scaling = jnp.repeat(block_scaling, TOK_DEV, axis=1)
    jaggedness = jnp.exp(jax.random.uniform(every_key[4], (HEAD_TOTAL, WINDOW_TOKENS), minval=-0.35, maxval=0.35))
    spike_locations = jax.random.randint(every_key[5], (3,), 0, WINDOW_TOKENS)
    spike_mask = jnp.any(jnp.arange(WINDOW_TOKENS)[None, :] == spike_locations[:, None], axis=0)
    spike_penalty = jax.random.uniform(every_key[6], (HEAD_TOTAL, WINDOW_TOKENS), minval=0.2, maxval=0.35)
    spike_dropout = jnp.where(spike_mask[None, :], jnp.log(1.0 - spike_penalty), 0.0)
    return (spike_dropout - baseline_rate * block_scaling * jaggedness).astype(jnp.float32)


def place_ends(result, key, smallest, largest):
    longest = result.shape.index(max(result.shape))
    spots = []
    for shift in (0, 1):
        where = [jax.random.randint(jax.random.fold_in(key, axis), (), 0, length) for axis, length in enumerate(result.shape)]
        where[longest] = (where[longest] + shift) % result.shape[longest]
        spots.append(tuple(where))
    return result.at[spots[0]].set(smallest).at[spots[1]].set(largest)


def shard_levels(key, dims, cuts, smallest, largest):
    factor_of, own = 1.0, jax.random.fold_in(key, 6)
    for dim, blocks in cuts:
        steps = jnp.exp(jax.random.uniform(jax.random.fold_in(own, dim), (blocks,), jnp.float32, smallest / len(cuts), largest / len(cuts)))
        factor_of = factor_of * jnp.repeat(steps, dims[dim] // blocks).reshape([-1 if axis == dim else 1 for axis in range(len(dims))])
    return factor_of


def normal_values(rng, extent, scale, reach, cuts=(), kind=jnp.bfloat16):
    loudness = shard_levels(rng, extent, cuts, -0.22, 0.18) if cuts else 1.0
    drawn = jax.random.normal(rng, extent, jnp.float32) * scale * loudness
    return jnp.minimum(jnp.maximum(drawn, -reach), reach).astype(kind)


def setup_inputs(seed: int = 0) -> dict:
    arg_keys = jax.random.split(jax.random.key(seed), 7)
    return {
        "queries": normal_values(arg_keys[0], (WINDOW_TOKENS, HEAD_TOTAL * HEAD_DIM), HEAD_DIM ** -0.5, 0.5, ((0, 8), (1, 4))),
        "keys": normal_values(arg_keys[1], (WINDOW_TOKENS, HEAD_TOTAL * HEAD_DIM), 1.0, 6.0, ((0, 8), (1, 4))),
        "values": normal_values(arg_keys[2], (WINDOW_TOKENS, HEAD_TOTAL * HEAD_DIM), 1.0, 6.0, ((0, 8), (1, 4))),
        "cotangent": normal_values(arg_keys[3], (WINDOW_TOKENS, HEAD_TOTAL * HEAD_DIM), 1.0, 6.0, ((0, 8), (1, 4))),
        "log_decay": draw_log_decay(jax.random.fold_in(arg_keys[6], 71), 0),
        "starts": place_ends((jax.random.randint(arg_keys[5], (WINDOW_TOKENS,), 0, WINDOW_TOKENS // 4) < 1).astype(jnp.int32), jax.random.fold_in(arg_keys[5], 1), 0, 1),
    }


EPS = 1e-05

def rounded(array):
    return lax.optimization_barrier(array.astype(jnp.bfloat16)).astype(jnp.float32)

def block_factors(log_rates, start_flags):
    cum_log = jnp.cumsum(log_rates, axis=1)
    doc_count = jnp.cumsum(start_flags.astype(jnp.int32))
    length = start_flags.shape[0]
    position = jnp.arange(length, dtype=jnp.int32)
    inside = (position[:, None] >= position[None, :]) & (doc_count[:, None] == doc_count[None, :])
    gap = cum_log[:, :, None] - cum_log[:, None, :]
    weight = jnp.where(inside[None], jnp.exp(jnp.minimum(gap, 0.0)), 0.0)
    entering = jnp.where(doc_count[None, :] == 0, jnp.exp(cum_log), 0.0)
    leaving = jnp.where(doc_count[None, :] == doc_count[-1], jnp.exp(cum_log[:, -1:] - cum_log), 0.0)
    carried = jnp.where(doc_count[-1] == 0, jnp.exp(cum_log[:, -1]), 0.0)
    return (weight, entering, leaving, carried)

def reference(queries, keys, values, cotangent, log_decay, starts):
    token_count, row_width = queries.shape
    head_count = log_decay.shape[0]
    head_dim = row_width // head_count
    block_count = token_count // TOK_DEV

    def blocks_of(array):
        return array.reshape(block_count, TOK_DEV, head_count, head_dim)
    query_blocks = blocks_of(queries)
    key_blocks = blocks_of(keys)
    value_blocks = blocks_of(values)
    cotangent_blocks = blocks_of(cotangent)
    log_blocks = log_decay.reshape(head_count, block_count, TOK_DEV).transpose(1, 0, 2)
    start_blocks = starts.reshape(block_count, TOK_DEV)

    def forward(state, pieces):
        query_head, key_head, value_head, cotangent_head, log_rates, start_flags = pieces
        weight, entering, leaving, carried = block_factors(log_rates, start_flags)
        query_wide = query_head.astype(jnp.float32)
        key_wide = key_head.astype(jnp.float32)
        value_wide = value_head.astype(jnp.float32)
        cotangent_wide = cotangent_head.astype(jnp.float32)
        weights_rounded = rounded(jnp.einsum('thd,shd->hts', query_wide, key_wide) * weight)
        state_rounded = rounded(state)
        outputs = jnp.einsum('hts,shd->thd', weights_rounded, value_wide)
        outputs = outputs + entering.T[:, :, None] * jnp.einsum('thd,hde->the', query_wide, state_rounded)
        keys_decayed = rounded(leaving.T[:, :, None] * key_wide)
        update = rounded(jnp.einsum('shd,she->hde', keys_decayed, value_wide))
        inverse_scale = lax.rsqrt(lax.optimization_barrier(jnp.sum(outputs * outputs, axis=(1, 2))) / row_width + EPS)
        attn_block = (outputs * inverse_scale[:, None, None]).astype(jnp.bfloat16)
        grad_sum = lax.optimization_barrier(jnp.sum(cotangent_wide * outputs, axis=(1, 2)))
        cubed = inverse_scale * inverse_scale * inverse_scale
        grad_out = rounded(inverse_scale[:, None, None] * cotangent_wide - (cubed * grad_sum / row_width)[:, None, None] * outputs)
        queries_decayed = rounded(entering.T[:, :, None] * query_wide)
        grad_state = rounded(jnp.einsum('thd,the->hde', queries_decayed, grad_out))
        next_state = carried[:, None, None] * state + update
        return (next_state, (attn_block, grad_out.astype(jnp.bfloat16), state_rounded, grad_state, carried))
    initial = jnp.zeros((head_count, head_dim, head_dim), jnp.float32)
    final_state, stacked = lax.scan(forward, initial, (query_blocks, key_blocks, value_blocks, cotangent_blocks, log_blocks, start_blocks))
    attn_blocks, grad_out_blocks, state_blocks, grad_states, carry_blocks = stacked

    def backward_carry(back, pieces):
        grad_state, carried = pieces
        return (grad_state + carried[:, None, None] * back, back)
    final_back, back_blocks = lax.scan(backward_carry, initial, (grad_states, carry_blocks), reverse=True)

    def backward(pieces):
        query_head, key_head, value_head, log_rates, start_flags, grad_out, state_rounded, back = pieces
        weight, entering, leaving, carried = block_factors(log_rates, start_flags)
        query_wide = query_head.astype(jnp.float32)
        key_wide = key_head.astype(jnp.float32)
        value_wide = value_head.astype(jnp.float32)
        grad_wide = grad_out.astype(jnp.float32)
        weights_rounded = rounded(jnp.einsum('thd,shd->hts', query_wide, key_wide) * weight)
        grads_rounded = rounded(jnp.einsum('thd,shd->hts', grad_wide, value_wide) * weight)
        back_rounded = rounded(back)
        grad_query = jnp.einsum('hts,shd->thd', grads_rounded, key_wide)
        grad_query = grad_query + entering.T[:, :, None] * jnp.einsum('the,hde->thd', grad_wide, state_rounded)
        grad_key = jnp.einsum('hts,thd->shd', grads_rounded, query_wide)
        grad_key = grad_key + leaving.T[:, :, None] * jnp.einsum('she,hde->shd', value_wide, back_rounded)
        grad_value = jnp.einsum('hts,thd->shd', weights_rounded, grad_wide)
        grad_value = grad_value + leaving.T[:, :, None] * jnp.einsum('shd,hde->she', key_wide, back_rounded)
        return (grad_query.astype(jnp.bfloat16), grad_key.astype(jnp.bfloat16), grad_value.astype(jnp.bfloat16))
    grad_query, grad_key, grad_value = lax.map(backward, (query_blocks, key_blocks, value_blocks, log_blocks, start_blocks, grad_out_blocks, state_blocks, back_blocks))
    return (attn_blocks.reshape(token_count, row_width), grad_query.reshape(token_count, row_width), grad_key.reshape(token_count, row_width), grad_value.reshape(token_count, row_width))
```

```python
import functools

import jax
import jax.numpy as jnp
from jax import lax
from jax.experimental import pallas as pl
from jax.experimental.pallas import tpu as pltpu
from jax.sharding import PartitionSpec as P

HEAD_TOTAL = 64
HEAD_DIM = 128
EPS = 1e-05
LOG2E = 1.4426950408889634
MASKED = -1e30
ROWS = 16
HALF = 256
F32 = jnp.float32
BF16 = jnp.bfloat16


def dot(a, b, dims=((1,), (0,))):
    return lax.dot_general(a, b, (dims, ((), ())), preferred_element_type=F32)


def dot_nt(a, b):
    return dot(a, b, ((1,), (1,)))


def running_sum(x):
    width = x.shape[1]
    lane = lax.broadcasted_iota(jnp.int32, x.shape, 1)
    step = 1
    while step < width:
        x = x + jnp.where(lane >= step, pltpu.roll(x, step, 1), 0.0)
        step *= 2
    return x


def three_parts(x):
    high = x.astype(BF16).astype(F32)
    rest = x - high
    middle = rest.astype(BF16).astype(F32)
    return high, middle, rest - middle


def block_mask(table, transposed):
    length = table.shape[1]
    row = table[ROWS - 1 :, :]
    column = table.T[:, ROWS - 1 :]
    down = lax.broadcasted_iota(jnp.int32, (length, length), 0)
    across = lax.broadcasted_iota(jnp.int32, (length, length), 1)
    order = (across >= down) if transposed else (down >= across)
    return jnp.where(order & (row == column), 0.0, MASKED)


def update_kernel(group, hpo, logs_ref, starts_ref, k_ref, v_ref, payload_ref, table_ref):
    step = pl.program_id(0)
    heads, length = logs_ref.shape
    dim = k_ref.shape[1] // group

    @pl.when(step == 0)
    def _():
        logs = running_sum(logs_ref[...]) * LOG2E
        count = running_sum(jnp.broadcast_to(starts_ref[...].astype(F32), (8, length)))[:1]
        enter = jnp.where(count == 0.0, jnp.exp2(logs), 0.0)
        last = slice(length - 1, length)
        leave = jnp.where(count == count[:, last], jnp.exp2(logs[:, last] - logs), 0.0)
        fill = jnp.broadcast_to(count, (ROWS - 3 * group, length))
        for g in range(heads // group):
            rows = slice(g * group, (g + 1) * group)
            table_ref[g] = jnp.concatenate([logs[rows], enter[rows], leave[rows], fill], axis=0)

    table = table_ref[step]
    columns = table.T
    carry = jnp.broadcast_to(table[group : 2 * group, length - 1 :], (group, dim))
    parts = three_parts(carry)
    line = lax.broadcasted_iota(jnp.int32, (ROWS, dim), 0)
    for owner in range(group // hpo):
        tile = jnp.zeros((ROWS, dim), F32)
        for i in range(hpo):
            h = owner * hpo + i
            lanes = slice(h * dim, (h + 1) * dim)
            decayed = (columns[:, 2 * group + h : 2 * group + h + 1] * k_ref[:, lanes].astype(F32)).astype(BF16)
            update = dot(decayed.T, v_ref[:, lanes])
            payload_ref[owner, i * dim : (i + 1) * dim, :] = update.astype(BF16)
            for j, part in enumerate(parts):
                tile = jnp.where(line == 3 * i + j, part[h : h + 1], tile)
        payload_ref[owner, hpo * dim :, :] = tile.astype(BF16)


def forward_scan_kernel(hpo, dim, in_ref, out_ref, carry_ref):
    state = [jnp.zeros((dim, dim), F32) for _ in range(hpo)]
    for b in range(in_ref.shape[0]):
        tile = in_ref[b, hpo * dim :, :].astype(F32)
        for i in range(hpo):
            rows = slice(i * dim, (i + 1) * dim)
            carry = tile[3 * i : 3 * i + 1] + tile[3 * i + 1 : 3 * i + 2] + tile[3 * i + 2 : 3 * i + 3]
            carry_ref[b, i : i + 1, :] = carry
            out_ref[b, rows, :] = state[i].astype(BF16)
            state[i] = carry * state[i] + in_ref[b, rows, :].astype(F32)


def backward_scan_kernel(hpo, dim, in_ref, carry_ref, out_ref):
    state = [jnp.zeros((dim, dim), F32) for _ in range(hpo)]
    for b in reversed(range(in_ref.shape[0])):
        for i in range(hpo):
            rows = slice(i * dim, (i + 1) * dim)
            out_ref[b, rows, :] = state[i].astype(BF16)
            state[i] = carry_ref[b, i : i + 1, :] * state[i] + in_ref[b, rows, :].astype(F32)


def intra_kernel(group, table_ref, q_ref, k_ref, v_ref, out_ref, mask_ref):
    length = q_ref.shape[0]
    dim = q_ref.shape[1] // group
    table = table_ref[0]

    @pl.when(pl.program_id(0) == 0)
    def _():
        mask_ref[...] = block_mask(table, False)

    columns = table.T
    for h in range(group):
        lanes = slice(h * dim, (h + 1) * dim)
        for first in range(0, length, HALF):
            rows, seen = slice(first, first + HALF), slice(0, first + HALF)
            scores = dot_nt(q_ref[rows, lanes], k_ref[seen, lanes])
            gap = columns[rows, h : h + 1] - table[h : h + 1, seen]
            weight = jnp.exp2(gap + mask_ref[rows, seen])
            out_ref[rows, lanes] = dot((scores * weight).astype(BF16), v_ref[seen, lanes])


def token_rows(total):
    length = total.shape[0]
    return jnp.concatenate(
        [jnp.sum(total[i : i + 128].T, axis=0, keepdims=True) for i in range(0, length, 128)], axis=0
    )


def output_kernel(group, table_ref, q_ref, state_ref, intra_ref, cot_ref, out_ref, sums_ref, square_ref, cross_ref):
    step = pl.program_id(0)
    dim = q_ref.shape[1] // group
    columns = table_ref[0].T

    @pl.when(step == 0)
    def _():
        square_ref[...] = jnp.zeros_like(square_ref)
        cross_ref[...] = jnp.zeros_like(cross_ref)

    square, cross = square_ref[...], cross_ref[...]
    for h in range(group):
        lanes = slice(h * dim, (h + 1) * dim)
        carried = dot(q_ref[:, lanes], state_ref[h])
        out = intra_ref[:, lanes] + columns[:, group + h : group + h + 1] * carried
        out_ref[:, lanes] = out
        square = square + out * out
        cross = cross + cot_ref[:, lanes].astype(F32) * out
    square_ref[...] = square
    cross_ref[...] = cross

    @pl.when(step == pl.num_programs(0) - 1)
    def _():
        sums_ref[...] = jnp.concatenate([token_rows(square), token_rows(cross)], axis=0)


def gout_kernel(group, hpo, count, *refs):
    sums_refs, refs = refs[:count], refs[count:]
    table_ref, q_ref, out_ref, cot_ref, attn_ref, gout_ref, payload_ref, factor_ref = refs
    dim = q_ref.shape[1] // group
    columns = table_ref[0].T

    @pl.when(pl.program_id(0) == 0)
    def _():
        total = sums_refs[0][...]
        for ref in sums_refs[1:]:
            total = total + ref[...]
        lines = total.shape[0] // 2
        full = HEAD_TOTAL * HEAD_DIM
        scale = lax.rsqrt(total[:lines] / full + EPS)
        slope = scale * scale * scale * total[lines:] / full
        turned = jnp.concatenate([scale, slope], axis=0).T
        for i in range(lines):
            rows = slice(i * 128, (i + 1) * 128)
            factor_ref[rows, 0:1] = turned[:, i : i + 1]
            factor_ref[rows, 1:2] = turned[:, lines + i : lines + i + 1]

    scale = factor_ref[:, 0:1]
    slope = factor_ref[:, 1:2]
    for h in range(group):
        lanes = slice(h * dim, (h + 1) * dim)
        out = out_ref[:, lanes]
        attn_ref[:, lanes] = (out * scale).astype(BF16)
        gout = (scale * cot_ref[:, lanes].astype(F32) - slope * out).astype(BF16)
        gout_ref[:, lanes] = gout
        decayed = (columns[:, group + h : group + h + 1] * q_ref[:, lanes].astype(F32)).astype(BF16)
        update = dot(decayed.T, gout)
        payload_ref[h // hpo, (h % hpo) * dim : (h % hpo + 1) * dim, :] = update.astype(BF16)


def gradient_kernel(group, table_ref, q_ref, k_ref, v_ref, gout_ref, state_ref, gq_ref, gk_ref, gv_ref, mask_ref):
    length = q_ref.shape[0]
    dim = q_ref.shape[1] // group
    table = table_ref[0]

    @pl.when(pl.program_id(0) == 0)
    def _():
        mask_ref[...] = block_mask(table, True)

    columns = table.T
    for h in range(group):
        lanes = slice(h * dim, (h + 1) * dim)
        pieces = []
        for first in range(0, length, HALF):
            rows, later = slice(first, first + HALF), slice(first, length)
            key, value = k_ref[rows, lanes], v_ref[rows, lanes]
            query, gout = q_ref[later, lanes], gout_ref[later, lanes]
            gap = table[h : h + 1, later] - columns[rows, h : h + 1]
            weight = jnp.exp2(gap + mask_ref[rows, later])
            probs = (dot_nt(key, query) * weight).astype(BF16)
            gv_ref[rows, lanes] = dot(probs, gout)
            grads = (dot_nt(value, gout) * weight).astype(BF16)
            gk_ref[rows, lanes] = dot(grads, query)
            pieces.append(dot(key.T, grads))
        carried = dot_nt(gout_ref[:, lanes], state_ref[h])
        for first in range(0, length, HALF):
            rows = slice(first, first + HALF)
            total = pieces[0][:, first : first + HALF]
            for i in range(1, first // HALF + 1):
                total = total + pieces[i][:, first - i * HALF : first - (i - 1) * HALF]
            enter = columns[rows, group + h : group + h + 1]
            gq_ref[rows, lanes] = (total.T + enter * carried[rows]).astype(BF16)


def final_kernel(group, table_ref, k_ref, v_ref, back_ref, gkp_ref, gvp_ref, gk_ref, gv_ref):
    dim = k_ref.shape[1] // group
    columns = table_ref[0].T
    for h in range(group):
        lanes = slice(h * dim, (h + 1) * dim)
        leave = columns[:, 2 * group + h : 2 * group + h + 1]
        gk_ref[:, lanes] = (gkp_ref[:, lanes] + leave * dot_nt(v_ref[:, lanes], back_ref[h])).astype(BF16)
        gv_ref[:, lanes] = (gvp_ref[:, lanes] + leave * dot(k_ref[:, lanes], back_ref[h])).astype(BF16)


def per_device(queries, keys, values, cotangent, log_decay, starts):
    length, width = queries.shape
    heads = log_decay.shape[0]
    dim = width // heads
    blocks = lax.axis_size("seq")
    shares = lax.axis_size("head")
    hpo = -(-heads // blocks)
    group = min(4, heads)
    groups = heads // group
    params = pltpu.CompilerParams(dimension_semantics=("arbitrary",), vmem_limit_bytes=48 << 20)

    wide = pl.BlockSpec((length, group * dim), lambda g: (0, g))
    table_spec = pl.BlockSpec((1, ROWS, length), lambda g: (g, 0, 0))
    state_spec = pl.BlockSpec((group, dim, dim), lambda g: (g, 0, 0))

    def whole(*shape):
        return pl.BlockSpec(shape, lambda g: (0,) * len(shape))

    def array(dtype):
        return jax.ShapeDtypeStruct((length, width), dtype)

    def cost(products, moved, exps=0):
        return pl.CostEstimate(flops=2 * heads * products, bytes_accessed=moved * length * width, transcendentals=heads * exps)

    big, small = length * length * dim, length * dim * dim
    payload, table = pl.pallas_call(
        functools.partial(update_kernel, group, hpo),
        grid=(groups,),
        in_specs=[whole(heads, length), whole(1, length), wide, wide],
        out_specs=[
            pl.BlockSpec((group // hpo, hpo * dim + ROWS, dim), lambda g: (g, 0, 0)),
            whole(groups, ROWS, length),
        ],
        out_shape=[
            jax.ShapeDtypeStruct((blocks, hpo * dim + ROWS, dim), BF16),
            jax.ShapeDtypeStruct((groups, ROWS, length), F32),
        ],
        compiler_params=params,
        cost_estimate=cost(small, 4),
        name="update",
    )(log_decay, starts.reshape(1, length), keys, values)

    received = lax.all_to_all(payload, "seq", 0, 0)

    intra = pl.pallas_call(
        functools.partial(intra_kernel, group),
        grid=(groups,),
        in_specs=[table_spec, wide, wide, wide],
        out_specs=wide,
        out_shape=array(F32),
        scratch_shapes=[pltpu.VMEM((length, length), F32)],
        compiler_params=params,
        cost_estimate=cost(2 * big, 10, length * length),
        name="intra",
    )(table, queries, keys, values)

    states, carries = pl.pallas_call(
        functools.partial(forward_scan_kernel, hpo, dim),
        out_shape=[
            jax.ShapeDtypeStruct((blocks, hpo * dim, dim), BF16),
            jax.ShapeDtypeStruct((blocks, 8, dim), F32),
        ],
        compiler_params=pltpu.CompilerParams(vmem_limit_bytes=48 << 20),
        name="forward_scan",
    )(received)
    states = lax.all_to_all(states, "seq", 0, 0).reshape(blocks * hpo, dim, dim)

    lines = 2 * length // 128
    outputs, sums = pl.pallas_call(
        functools.partial(output_kernel, group),
        grid=(groups,),
        in_specs=[table_spec, wide, state_spec, wide, wide],
        out_specs=[wide, whole(lines, 128)],
        out_shape=[array(F32), jax.ShapeDtypeStruct((lines, 128), F32)],
        scratch_shapes=[pltpu.VMEM((length, dim), F32)] * 2,
        compiler_params=params,
        cost_estimate=cost(small, 12),
        name="output",
    )(table, queries, states, intra, cotangent)

    everyone = [sums] + [
        lax.ppermute(sums, "head", [(i, (i + k) % shares) for i in range(shares)]) for k in range(1, shares)
    ]

    attn, gout, payload = pl.pallas_call(
        functools.partial(gout_kernel, group, hpo, shares),
        grid=(groups,),
        in_specs=[whole(lines, 128)] * shares + [table_spec, wide, wide, wide],
        out_specs=[wide, wide, pl.BlockSpec((group // hpo, hpo * dim, dim), lambda g: (g, 0, 0))],
        out_shape=[array(BF16), array(BF16), jax.ShapeDtypeStruct((blocks, hpo * dim, dim), BF16)],
        scratch_shapes=[pltpu.VMEM((length, 2), F32)],
        compiler_params=params,
        cost_estimate=cost(small, 12),
        name="gout",
    )(*everyone, table, queries, outputs, cotangent)

    received = lax.all_to_all(payload, "seq", 0, 0)

    gq, gk_part, gv_part = pl.pallas_call(
        functools.partial(gradient_kernel, group),
        grid=(groups,),
        in_specs=[table_spec, wide, wide, wide, wide, state_spec],
        out_specs=[wide, wide, wide],
        out_shape=[array(BF16), array(F32), array(F32)],
        scratch_shapes=[pltpu.VMEM((length, length), F32)],
        compiler_params=params,
        cost_estimate=cost(5 * big + small, 18, length * length),
        name="gradient",
    )(table, queries, keys, values, gout, states)

    back = pl.pallas_call(
        functools.partial(backward_scan_kernel, hpo, dim),
        out_shape=jax.ShapeDtypeStruct((blocks, hpo * dim, dim), BF16),
        compiler_params=pltpu.CompilerParams(vmem_limit_bytes=48 << 20),
        name="backward_scan",
    )(received, carries)
    back = lax.all_to_all(back, "seq", 0, 0).reshape(blocks * hpo, dim, dim)

    gk, gv = pl.pallas_call(
        functools.partial(final_kernel, group),
        grid=(groups,),
        in_specs=[table_spec, wide, wide, state_spec, wide, wide],
        out_specs=[wide, wide],
        out_shape=[array(BF16), array(BF16)],
        compiler_params=params,
        cost_estimate=cost(2 * small, 16),
        name="final",
    )(table, keys, values, back, gk_part, gv_part)
    return (attn, gq, gk, gv)


def solution(mesh):
    wide = P("seq", "head")
    return jax.shard_map(
        per_device,
        mesh=mesh,
        in_specs=(wide, wide, wide, wide, P("head", "seq"), P("seq")),
        out_specs=(wide, wide, wide, wide),
        check_vma=False,
    )
```

```python
import functools

import jax
import jax.numpy as jnp
from jax import lax
from jax.experimental import pallas as pl
from jax.experimental.pallas import tpu as pltpu
from jax.sharding import PartitionSpec as P

HEAD_TOTAL = 64
HEAD_DIM = 128
EPS = 1e-05
LOG2E = 1.4426950408889634
MASKED = -1e30
ROWS = 16
HALF = 256
F32 = jnp.float32
BF16 = jnp.bfloat16


def dot(a, b, dims=((1,), (0,))):
    return lax.dot_general(a, b, (dims, ((), ())), preferred_element_type=F32)


def dot_nt(a, b):
    return dot(a, b, ((1,), (1,)))


def running_sum(x):
    width = x.shape[1]
    lane = lax.broadcasted_iota(jnp.int32, x.shape, 1)
    step = 1
    while step < width:
        x = x + jnp.where(lane >= step, pltpu.roll(x, step, 1), 0.0)
        step *= 2
    return x


def three_parts(x):
    high = x.astype(BF16).astype(F32)
    rest = x - high
    middle = rest.astype(BF16).astype(F32)
    return high, middle, rest - middle


def lanes_of(index, size):
    return pl.ds(index * size if isinstance(index, int) else pl.multiple_of(index * size, size), size)


def send_to(place, slot, size):
    return place ^ slot if size & (size - 1) == 0 else lax.rem(place + slot, size)


def sent_by(place, slot, size):
    return place ^ slot if size & (size - 1) == 0 else lax.rem(place + size - slot, size)


def my_place(size):
    return lax.rem(lax.axis_index("seq"), size)


def block_mask(table, transposed):
    length = table.shape[1]
    row = table[ROWS - 1 :, :]
    column = table.T[:, ROWS - 1 :]
    down = lax.broadcasted_iota(jnp.int32, (length, length), 0)
    across = lax.broadcasted_iota(jnp.int32, (length, length), 1)
    order = (across >= down) if transposed else (down >= across)
    return jnp.where(order & (row == column), 0.0, MASKED)


def update_kernel(group, hpo, size, logs_hbm, starts_hbm, k_hbm, v_hbm, q_hbm, *refs):
    sent_refs, refs = refs[:size], refs[size:]
    table_ref, rows_ref, k_ref, v_ref, q_ref, logs_ref, starts_ref, sems = refs
    heads, length = logs_ref.shape
    dim = k_ref.shape[1] // heads
    pairs = ((logs_hbm, logs_ref), (starts_hbm, starts_ref), (k_hbm, k_ref), (v_hbm, v_ref), (q_hbm, q_ref))
    copies = [pltpu.make_async_copy(a, b, sems.at[i]) for i, (a, b) in enumerate(pairs)]
    for copy in copies[:4]:
        copy.start()
    copies[0].wait()
    copies[1].wait()

    flags = jnp.broadcast_to(starts_ref[...].astype(F32), (8, length))
    sums = running_sum(jnp.concatenate([logs_ref[...], flags], axis=0))
    logs, count = sums[:heads] * LOG2E, sums[heads : heads + 1]
    last = slice(length - 1, length)
    enter = jnp.where(count == 0.0, jnp.exp2(logs), 0.0)
    leave = jnp.where(count == count[:, last], jnp.exp2(logs[:, last] - logs), 0.0)
    fill = jnp.broadcast_to(count, (ROWS - 3 * group, length))
    for g in range(heads // group):
        rows = slice(g * group, (g + 1) * group)
        table_ref[g] = jnp.concatenate([logs[rows], enter[rows], leave[rows], fill], axis=0)
    for h in range(heads):
        rows_ref[h] = enter[h : h + 1]
        rows_ref[heads + h] = leave[h : h + 1]
    line = lax.broadcasted_iota(jnp.int32, (ROWS, dim), 0)
    copies[2].wait()
    copies[3].wait()
    copies[4].start()

    me = my_place(size)
    for slot, sent_ref in enumerate(sent_refs):
        owner = send_to(me, slot, size)

        @pl.when(owner * hpo < heads)
        def _():
            tile = jnp.zeros((ROWS, dim), F32)
            for i in range(hpo):
                head = owner * hpo + i
                lanes = lanes_of(head, dim)
                turned = k_ref[:, lanes].T.astype(F32)
                decayed = (turned * rows_ref[heads + head]).astype(BF16)
                sent_ref[i * dim : (i + 1) * dim, :] = dot(decayed, v_ref[:, lanes]).astype(BF16)
                carry = rows_ref[head][:, length - 1 :]
                for j, part in enumerate(three_parts(jnp.broadcast_to(carry, (ROWS, dim)))):
                    tile = jnp.where(line == 3 * i + j, part, tile)
            sent_ref[hpo * dim :, :] = tile.astype(BF16)

    copies[4].wait()


def scan_kernel(hpo, size, forward, *refs):
    in_refs, refs = refs[:size], refs[size:]
    if forward:
        _, local_ref, total_ref, factor_ref, carry_ref, ordered_ref = refs
    else:
        carry_ref, _, local_ref, total_ref, factor_ref, ordered_ref = refs
    dim = in_refs[0].shape[1]
    me = my_place(size)
    for slot, in_ref in enumerate(in_refs):
        ordered_ref[sent_by(me, slot, size)] = in_ref[...]
    if forward:
        for b in range(size):
            tile = ordered_ref[b, hpo * dim :, :].astype(F32)
            for i in range(hpo):
                carry_ref[b, i : i + 1, :] = tile[3 * i : 3 * i + 1] + tile[3 * i + 1 : 3 * i + 2] + tile[3 * i + 2 : 3 * i + 3]
    for i in range(hpo):
        rows = slice(i * dim, (i + 1) * dim)
        state = jnp.zeros((dim, dim), F32)
        factor = jnp.ones((1, dim), F32)
        for b in range(size) if forward else reversed(range(size)):
            carry = carry_ref[b, i : i + 1, :]
            local_ref[b, rows, :] = state
            factor_ref[b, i : i + 1, :] = factor
            state = carry * state + ordered_ref[b, rows, :].astype(F32)
            factor = factor * carry
        total_ref[rows, :] = state.astype(BF16)


def return_kernel(hpo, size, local_ref, factor_ref, outer_ref, _, *out_refs):
    dim = local_ref.shape[2]
    me = my_place(size)
    for i in range(hpo):
        rows = slice(i * dim, (i + 1) * dim)
        outer = outer_ref[rows, :].astype(F32)
        for slot, out_ref in enumerate(out_refs):
            b = send_to(me, slot, size)
            out_ref[rows, :] = (local_ref[b, rows, :] + factor_ref[b, i : i + 1, :] * outer).astype(BF16)


def ordered_states(hpo, size, state_ref, in_refs):
    dim = in_refs[0].shape[1]
    me = my_place(size)
    for slot, in_ref in enumerate(in_refs):
        owner = sent_by(me, slot, size)
        for i in range(hpo):
            state_ref[owner * hpo + i] = in_ref[i * dim : (i + 1) * dim, :]


def intra_kernel(group, dim, begin, end, table_ref, q_ref, k_ref, v_ref, *refs):
    length = q_ref.shape[0]
    copy = None
    if begin == 0:
        cot_hbm, out_ref, cot_ref, mask_ref, sems = refs
        copy = pltpu.make_async_copy(cot_hbm, cot_ref, sems.at[0])
        copy.start()
    else:
        out_ref, mask_ref = refs
    mask_ref[...] = block_mask(table_ref[0], False)

    def one(g, _):
        table = table_ref[g]
        columns = table.T
        for h in range(group):
            lanes = lanes_of(g * group + h, dim)
            local = lanes_of((g - begin) * group + h, dim)
            for first in range(0, length, HALF):
                rows, seen = pl.ds(first, HALF), pl.ds(0, first + HALF)
                scores = dot_nt(q_ref[rows, lanes], k_ref[seen, lanes])
                gap = columns[first : first + HALF, h : h + 1] - table[h : h + 1, : first + HALF]
                weight = jnp.exp2(gap + mask_ref[rows, seen])
                out_ref[rows, local] = dot((scores * weight).astype(BF16), v_ref[seen, lanes])
        return 0

    lax.fori_loop(begin, end, one, 0)
    if copy is not None:
        copy.wait()


def token_rows(total):
    length = total.shape[0]
    return jnp.concatenate(
        [jnp.sum(total[i : i + 128].T, axis=0, keepdims=True) for i in range(0, length, 128)], axis=0
    )


def output_kernel(group, hpo, size, cuts, table_ref, q_ref, cot_ref, *refs):
    intra_refs, refs = refs[: len(cuts)], refs[len(cuts) :]
    in_refs, refs = refs[:size], refs[size:]
    out_ref, state_ref, sums_ref, square_ref, cross_ref = refs
    dim = in_refs[0].shape[1]
    ordered_states(hpo, size, state_ref, in_refs)
    square_ref[...] = jnp.zeros_like(square_ref)
    cross_ref[...] = jnp.zeros_like(cross_ref)
    for (begin, end), intra_ref in zip(cuts, intra_refs):

        def one(g, _):
            columns = table_ref[g].T
            square, cross = square_ref[...], cross_ref[...]
            for h in range(group):
                lanes = lanes_of(g * group + h, dim)
                local = lanes_of((g - begin) * group + h, dim)
                carried = dot(q_ref[:, lanes], state_ref[g * group + h])
                out = intra_ref[:, local] + columns[:, group + h : group + h + 1] * carried
                out_ref[:, lanes] = out
                square = square + out * out
                cross = cross + cot_ref[:, lanes].astype(F32) * out
            square_ref[...] = square
            cross_ref[...] = cross
            return 0

        lax.fori_loop(begin, end, one, 0)
    sums_ref[...] = jnp.concatenate([token_rows(square_ref[...]), token_rows(cross_ref[...])], axis=0)


def gout_kernel(hpo, size, count, *refs):
    sums_refs, refs = refs[:count], refs[count:]
    rows_ref, q_ref, out_ref, cot_ref, attn_hbm, gout_ref = refs[:6]
    sent_refs, (attn_ref, factor_ref, sems) = refs[6 : 6 + size], refs[6 + size :]
    heads = rows_ref.shape[0] // 2
    dim = q_ref.shape[1] // heads
    total = sums_refs[0][...]
    for ref in sums_refs[1:]:
        total = total + ref[...]
    lines = total.shape[0] // 2
    full = HEAD_TOTAL * HEAD_DIM
    scale = lax.rsqrt(total[:lines] / full + EPS)
    slope = scale * scale * scale * total[lines:] / full
    turned = jnp.concatenate([scale, slope], axis=0).T
    for i in range(lines):
        rows = slice(i * 128, (i + 1) * 128)
        factor_ref[0, rows, :] = jnp.broadcast_to(turned[:, i : i + 1], (128, dim))
        factor_ref[1, rows, :] = jnp.broadcast_to(turned[:, lines + i : lines + i + 1], (128, dim))

    me = my_place(size)

    def store(slot):
        lanes = lanes_of(send_to(me, slot, size), hpo * dim)
        return pltpu.make_async_copy(attn_ref.at[:, lanes], attn_hbm.at[:, lanes], sems.at[slot])

    for slot, sent_ref in enumerate(sent_refs):
        owner = send_to(me, slot, size)

        @pl.when(owner * hpo < heads)
        def _():
            for i in range(hpo):
                head = owner * hpo + i
                lanes = lanes_of(head, dim)
                scale, slope = factor_ref[0], factor_ref[1]
                out = out_ref[:, lanes]
                attn_ref[:, lanes] = (scale * out).astype(BF16)
                gout = (scale * cot_ref[:, lanes].astype(F32) - slope * out).astype(BF16)
                gout_ref[:, lanes] = gout
                decayed = (q_ref[:, lanes].T.astype(F32) * rows_ref[head]).astype(BF16)
                sent_ref[i * dim : (i + 1) * dim, :] = dot(decayed, gout).astype(BF16)
            store(slot).start()

    for slot in range(size):

        @pl.when(send_to(me, slot, size) * hpo < heads)
        def _():
            store(slot).wait()


def gradient_kernel(group, dim, begin, end, table_ref, q_ref, k_ref, v_ref, gout_ref, state_ref, *refs):
    if begin > 0:
        refs = refs[1:]
    gq_hbm, gk_ref, gv_ref, gq_ref, mask_ref, sems = refs
    length = q_ref.shape[0]
    wide = group * dim
    mask_ref[...] = block_mask(table_ref[0], True)

    def store(g):
        return pltpu.make_async_copy(
            gq_ref.at[:, lanes_of(g - begin, wide)], gq_hbm.at[:, lanes_of(g, wide)], sems.at[g - begin]
        )

    def one(g, _):
        table = table_ref[g]
        columns = table.T
        for h in range(group):
            lanes = lanes_of(g * group + h, dim)
            local = lanes_of((g - begin) * group + h, dim)
            query_turned, gout_turned = q_ref[:, lanes].T, gout_ref[:, lanes].T
            carried = dot(state_ref[g * group + h], gout_turned)
            pieces = [table[group + h : group + h + 1] * carried]
            for first in range(0, length, HALF):
                rows, later = pl.ds(first, HALF), pl.ds(first, length - first)
                key, value = k_ref[rows, lanes], v_ref[rows, lanes]
                gap = table[h : h + 1, first:] - columns[first : first + HALF, h : h + 1]
                weight = jnp.exp2(gap + mask_ref[rows, later])
                probs = (dot(key, query_turned[:, first:]) * weight).astype(BF16)
                gv_ref[rows, local] = dot(probs, gout_ref[later, lanes])
                grads = (dot(value, gout_turned[:, first:]) * weight).astype(BF16)
                gk_ref[rows, local] = dot(grads, q_ref[later, lanes])
                pieces.append(dot(key.T, grads))
            for first in range(0, length, HALF):
                total = pieces[0][:, first : first + HALF]
                for i in range(first // HALF + 1):
                    total = total + pieces[i + 1][:, first - i * HALF : first - (i - 1) * HALF]
                gq_ref[first : first + HALF, local] = total.astype(BF16).T
        store(g).start()
        return 0

    lax.fori_loop(begin, end, one, 0)
    for g in range(begin, end):
        store(g).wait()


def final_kernel(group, hpo, size, cuts, table_ref, k_ref, v_ref, *refs):
    parts, refs = refs[: 2 * len(cuts)], refs[2 * len(cuts) :]
    in_refs, refs = refs[:size], refs[size:]
    gk_hbm, gv_hbm, gk_ref, gv_ref, back_ref, sems = refs
    dim = in_refs[0].shape[1]
    wide = group * dim
    ordered_states(hpo, size, back_ref, in_refs)

    def stores(g):
        lanes = lanes_of(g, wide)
        return (
            pltpu.make_async_copy(gk_ref.at[:, lanes], gk_hbm.at[:, lanes], sems.at[0, g]),
            pltpu.make_async_copy(gv_ref.at[:, lanes], gv_hbm.at[:, lanes], sems.at[1, g]),
        )

    for (begin, end), gkp_ref, gvp_ref in zip(cuts, parts[::2], parts[1::2]):

        def one(g, _):
            columns = table_ref[g].T
            for h in range(group):
                lanes = lanes_of(g * group + h, dim)
                local = lanes_of((g - begin) * group + h, dim)
                leave = columns[:, 2 * group + h : 2 * group + h + 1]
                back = back_ref[g * group + h]
                gk_ref[:, lanes] = (gkp_ref[:, local] + leave * dot_nt(v_ref[:, lanes], back)).astype(BF16)
                gv_ref[:, lanes] = (gvp_ref[:, local] + leave * dot(k_ref[:, lanes], back)).astype(BF16)
            for copy in stores(g):
                copy.start()
            return 0

        lax.fori_loop(begin, end, one, 0)
    for g in range(table_ref.shape[0]):
        for copy in stores(g):
            copy.wait()


def exchange(arrays, size, halves):
    def pairs(slot):
        return [
            (base + place, base + int(send_to(place, slot, size) if size & (size - 1) == 0 else (place + slot) % size))
            for base in range(0, halves * size, size)
            for place in range(size)
        ]

    return [arrays[0]] + [lax.ppermute(arrays[slot], "seq", pairs(slot)) for slot in range(1, size)]


def split(groups, parts):
    edges = [round(i * groups / parts) for i in range(parts + 1)]
    return [(a, b) for a, b in zip(edges, edges[1:]) if b > a]


def per_device(queries, keys, values, cotangent, log_decay, starts):
    length, width = queries.shape
    heads = log_decay.shape[0]
    dim = width // heads
    blocks = lax.axis_size("seq")
    shares = lax.axis_size("head")
    halves = 2 if blocks % 2 == 0 else 1
    size = blocks // halves
    hpo = -(-heads // size)
    group = min(4, heads)
    groups = heads // group
    params = pltpu.CompilerParams(vmem_limit_bytes=16 << 20)

    inside = pl.BlockSpec(memory_space=pltpu.VMEM)
    unused = pl.BlockSpec(memory_space=pl.ANY)
    hbm = pl.BlockSpec(memory_space=pltpu.HBM)
    dma = pltpu.SemaphoreType.DMA

    def outside(array):
        return pltpu.with_memory_space_constraint(array, pltpu.HBM)

    def held(columns, dtype):
        return pltpu.VMEM((length, columns), dtype)

    def cost(products, exps=0, share=1.0):
        return pl.CostEstimate(
            flops=int(2 * heads * products * share),
            bytes_accessed=int(length * width * share),
            transcendentals=int(heads * exps * share),
        )

    def scan(arrays, carries, after, later):
        forward = carries is None
        local = pltpu.VMEM((size, hpo * dim, dim), F32)
        factor = pltpu.VMEM((size, 8, dim), F32)
        total = pltpu.VMEM((hpo * dim, dim), BF16)
        local, total, factor, *rest = pl.pallas_call(
            functools.partial(scan_kernel, hpo, size, forward),
            in_specs=[inside] * (size if forward else size + 1) + [unused],
            out_specs=[inside] * (4 if forward else 3),
            out_shape=[local, total, factor] + ([factor] if forward else []),
            scratch_shapes=[pltpu.VMEM((size, *arrays[0].shape), BF16)],
            compiler_params=params,
            name="scan",
        )(*arrays, *([] if forward else [carries]), after)
        if halves == 2:
            pairs = [(i, i + size) if forward else (i + size, i) for i in range(size)]
            outer = lax.ppermute(total, "seq", pairs)
        else:
            outer = jnp.zeros_like(total)
        back = pl.pallas_call(
            functools.partial(return_kernel, hpo, size),
            in_specs=[inside] * 3 + [unused],
            out_specs=[inside] * size,
            out_shape=[pltpu.VMEM((hpo * dim, dim), BF16)] * size,
            compiler_params=params,
            name="return",
        )(local, factor, outer, later)
        return exchange(back, size, halves), (rest[0] if forward else None)

    big, small = length * length * dim, length * dim * dim
    queries, keys, values, cotangent = (outside(a) for a in (queries, keys, values, cotangent))
    *sent, table, rows, k, v, q = pl.pallas_call(
        functools.partial(update_kernel, group, hpo, size),
        in_specs=[hbm] * 5,
        out_specs=[inside] * (size + 5),
        out_shape=[pltpu.VMEM((hpo * dim + ROWS, dim), BF16)] * size
        + [pltpu.VMEM((groups, ROWS, length), F32), pltpu.VMEM((2 * heads, 1, length), F32)]
        + [held(width, BF16)] * 3,
        scratch_shapes=[pltpu.VMEM((heads, length), F32), pltpu.VMEM((1, length), jnp.int32), dma((5,))],
        compiler_params=params,
        cost_estimate=cost(small),
        name="update",
    )(outside(log_decay), outside(starts.reshape(1, length)), keys, values, queries)
    received = exchange(sent, size, halves)

    cuts = split(groups, 2)
    intras = []
    cot = None
    for begin, end in cuts:
        first = begin == 0
        intra, *rest = pl.pallas_call(
            functools.partial(intra_kernel, group, dim, begin, end),
            in_specs=[inside] * 4 + [hbm] * first,
            out_specs=[inside] * (1 + first),
            out_shape=[held((end - begin) * group * dim, F32)] + [held(width, BF16)] * first,
            scratch_shapes=[pltpu.VMEM((length, length), F32)] + [dma((1,))] * first,
            compiler_params=params,
            cost_estimate=cost(2 * big, length * length, (end - begin) / groups),
            name="intra",
        )(table, q, k, v, *([cotangent] if first else []))
        intras.append(intra)
        cot = rest[0] if first else cot

    received, carries = scan(received, None, intras[0], intras[-1])

    lines = 2 * length // 128
    outputs, states, sums = pl.pallas_call(
        functools.partial(output_kernel, group, hpo, size, cuts),
        in_specs=[inside] * (3 + len(cuts) + size),
        out_specs=[inside] * 3,
        out_shape=[held(width, F32), pltpu.VMEM((size * hpo, dim, dim), BF16), pltpu.VMEM((lines, 128), F32)],
        scratch_shapes=[held(dim, F32)] * 2,
        compiler_params=params,
        cost_estimate=cost(small),
        name="output",
    )(table, q, cot, *intras, *received)

    everyone = [sums] + [
        lax.ppermute(sums, "head", [(i, (i + k) % shares) for i in range(shares)]) for k in range(1, shares)
    ]

    attn, gout, *sent = pl.pallas_call(
        functools.partial(gout_kernel, hpo, size, shares),
        in_specs=[inside] * (shares + 4),
        out_specs=[hbm] + [inside] * (1 + size),
        out_shape=[pltpu.HBM((length, width), BF16), held(width, BF16)] + [pltpu.VMEM((hpo * dim, dim), BF16)] * size,
        scratch_shapes=[held(width, BF16), pltpu.VMEM((2, length, dim), F32), dma((size,))],
        compiler_params=params,
        cost_estimate=cost(small),
        name="gout",
    )(*everyone, rows, q, outputs, cot)
    received = exchange(sent, size, halves)

    cuts = split(groups, 3)
    parts = []
    gq = None
    for begin, end in cuts:
        span = (end - begin) * group * dim
        gq, *rest = pl.pallas_call(
            functools.partial(gradient_kernel, group, dim, begin, end),
            in_specs=[inside] * 6 + [hbm] * (begin > 0),
            out_specs=[hbm] + [inside] * 2,
            out_shape=[pltpu.HBM((length, width), BF16)] + [held(span, F32)] * 2,
            scratch_shapes=[held(span, BF16), pltpu.VMEM((length, length), F32), dma((end - begin,))],
            input_output_aliases={6: 0} if begin > 0 else {},
            compiler_params=params,
            cost_estimate=cost(5 * big + small, length * length, (end - begin) / groups),
            name="gradient",
        )(table, q, k, v, gout, states, *([gq] if begin > 0 else []))
        parts += rest

    received, _ = scan(received, carries, parts[0], parts[-3 if len(cuts) > 2 else 0])

    gk, gv = pl.pallas_call(
        functools.partial(final_kernel, group, hpo, size, cuts),
        in_specs=[inside] * (3 + 2 * len(cuts) + size),
        out_specs=[hbm] * 2,
        out_shape=[pltpu.HBM((length, width), BF16)] * 2,
        scratch_shapes=[held(width, BF16)] * 2 + [pltpu.VMEM((size * hpo, dim, dim), BF16), dma((2, groups))],
        compiler_params=params,
        cost_estimate=cost(2 * small),
        name="final",
    )(table, k, v, *parts, *received)
    return (attn, gq, gk, gv)


def solution(mesh):
    wide = P("seq", "head")
    return jax.shard_map(
        per_device,
        mesh=mesh,
        in_specs=(wide, wide, wide, wide, P("head", "seq"), P("seq")),
        out_specs=(wide, wide, wide, wide),
        check_vma=False,
    )
```

```python
import functools

import jax
import jax.numpy as jnp
from jax import lax
from jax.experimental import pallas as pl
from jax.experimental.pallas import tpu as pltpu
from jax.sharding import PartitionSpec as P

HEAD_TOTAL = 64
HEAD_DIM = 128
EPS = 1e-05
LOG2E = 1.4426950408889634
MASKED = -1e30
ROWS = 16
HALF = 256
F32 = jnp.float32
BF16 = jnp.bfloat16


def dot(a, b, dims=((1,), (0,))):
    return lax.dot_general(a, b, (dims, ((), ())), preferred_element_type=F32)


def dot_nt(a, b):
    return dot(a, b, ((1,), (1,)))


def running_sum(x):
    width = x.shape[1]
    lane = lax.broadcasted_iota(jnp.int32, x.shape, 1)
    step = 1
    while step < width:
        x = x + jnp.where(lane >= step, pltpu.roll(x, step, 1), 0.0)
        step *= 2
    return x


def three_parts(x):
    high = x.astype(BF16).astype(F32)
    rest = x - high
    middle = rest.astype(BF16).astype(F32)
    return high, middle, rest - middle


def lanes_of(index, size):
    return pl.ds(index * size if isinstance(index, int) else pl.multiple_of(index * size, size), size)


def partner(place, slot, size):
    return place ^ slot if size & (size - 1) == 0 else (place + slot) % size


def inverse(place, slot, size):
    return place ^ slot if size & (size - 1) == 0 else (place + size - slot) % size


def my_place(size):
    return lax.rem(lax.axis_index("seq"), size)


def block_mask(table):
    length = table.shape[1]
    row = table[ROWS - 1 :, :]
    column = table.T[:, ROWS - 1 :]
    down = lax.broadcasted_iota(jnp.int32, (length, length), 0)
    across = lax.broadcasted_iota(jnp.int32, (length, length), 1)
    return jnp.where((across >= down) & (row == column), 0.0, MASKED)


class Plan:
    def __init__(self, heads, dim, length, size):
        self.heads, self.dim, self.length, self.size = heads, dim, length, size
        self.hpo = -(-heads // size)
        self.span = self.hpo * dim

    def lanes(self, slot):
        start = partner(my_place(self.size), slot, self.size) * self.span
        return pl.ds(pl.multiple_of(start, self.span), self.span)

    def head(self, i):
        return slice(i * self.dim, (i + 1) * self.dim)

    def guard(self, slot):
        if self.hpo * self.size == self.heads:
            return lambda body: body()
        return pl.when(partner(my_place(self.size), slot, self.size) * self.hpo < self.heads)


def order(size):
    return list(range(1, size)) + [0]


def update_kernel(plan, logs_hbm, starts_hbm, k_hbm, v_hbm, *refs):
    size, hpo, dim, heads = plan.size, plan.hpo, plan.dim, plan.heads
    sent_refs, k_refs, v_refs, turned_refs = (refs[i * size : (i + 1) * size] for i in range(4))
    table_ref, logs_ref, starts_ref, natural_ref, small_sems, sems = refs[4 * size :]
    length = plan.length
    copies = [
        pltpu.make_async_copy(logs_hbm, logs_ref, small_sems.at[0]),
        pltpu.make_async_copy(starts_hbm, starts_ref, small_sems.at[1]),
    ]
    for copy in copies:
        copy.start()

    def loads(slot):
        lanes = plan.lanes(slot)
        return (
            pltpu.make_async_copy(k_hbm.at[:, lanes], k_refs[slot], sems.at[0, slot]),
            pltpu.make_async_copy(v_hbm.at[:, lanes], v_refs[slot], sems.at[1, slot]),
        )

    for slot in order(size):

        @plan.guard(slot)
        def _():
            for copy in loads(slot):
                copy.start()

    for copy in copies:
        copy.wait()
    flags = jnp.broadcast_to(starts_ref[...].astype(F32), (8, length))
    sums = running_sum(jnp.concatenate([logs_ref[...], flags], axis=0))
    logs, count = sums[:heads] * LOG2E, sums[heads : heads + 1]
    last = slice(length - 1, length)
    enter = jnp.where(count == 0.0, jnp.exp2(logs), 0.0)
    leave = jnp.where(count == count[:, last], jnp.exp2(logs[:, last] - logs), 0.0)
    fill = jnp.broadcast_to(count, (ROWS - 3 * hpo, length))
    for owner in range(heads // hpo):
        rows = slice(owner * hpo, (owner + 1) * hpo)
        natural_ref[owner] = jnp.concatenate([logs[rows], enter[rows], leave[rows], fill], axis=0)
    line = lax.broadcasted_iota(jnp.int32, (ROWS, dim), 0)

    for slot in order(size):

        @plan.guard(slot)
        def _():
            table = natural_ref[partner(my_place(size), slot, size)]
            table_ref[slot] = table
            for copy in loads(slot):
                copy.wait()
            tile = jnp.zeros((ROWS, dim), F32)
            for i in range(hpo):
                lanes = plan.head(i)
                turned = k_refs[slot][:, lanes].T
                turned_refs[slot][lanes, :] = turned
                decayed = (turned.astype(F32) * table[2 * hpo + i : 2 * hpo + i + 1]).astype(BF16)
                sent_refs[slot][lanes, :] = dot(decayed, v_refs[slot][:, lanes]).astype(BF16)
                carry = jnp.broadcast_to(table[hpo + i : hpo + i + 1, last], (ROWS, dim))
                for j, part in enumerate(three_parts(carry)):
                    tile = jnp.where(line == 3 * i + j, part, tile)
            sent_refs[slot][hpo * dim :, :] = tile.astype(BF16)


def scan_kernel(plan, forward, *refs):
    size, hpo, dim = plan.size, plan.hpo, plan.dim
    in_refs, refs = refs[:size], refs[size:]
    if forward:
        local_ref, total_ref, factor_ref, carry_ref, ordered_ref = refs[-5:]
    else:
        carry_ref = refs[0]
        local_ref, total_ref, factor_ref, ordered_ref = refs[-4:]
    me = my_place(size)
    for slot, in_ref in enumerate(in_refs):
        ordered_ref[inverse(me, slot, size)] = in_ref[...]
    if forward:
        for b in range(size):
            tile = ordered_ref[b, hpo * dim :, :].astype(F32)
            for i in range(hpo):
                carry_ref[b, i : i + 1, :] = tile[3 * i : 3 * i + 1] + tile[3 * i + 1 : 3 * i + 2] + tile[3 * i + 2 : 3 * i + 3]
    for i in range(hpo):
        rows = plan.head(i)
        state = jnp.zeros((dim, dim), F32)
        factor = jnp.ones((1, dim), F32)
        for b in range(size) if forward else reversed(range(size)):
            carry = carry_ref[b, i : i + 1, :]
            local_ref[b, rows, :] = state
            factor_ref[b, i : i + 1, :] = factor
            state = carry * state + ordered_ref[b, rows, :].astype(F32)
            factor = factor * carry
        total_ref[rows, :] = state.astype(BF16)


def return_kernel(plan, local_ref, factor_ref, outer_ref, *refs):
    out_refs = refs[-plan.size :]
    me = my_place(plan.size)
    for i in range(plan.hpo):
        rows = plan.head(i)
        outer = outer_ref[rows, :].astype(F32)
        for slot, out_ref in enumerate(out_refs):
            b = inverse(me, slot, plan.size)
            out_ref[rows, :] = (local_ref[b, rows, :] + factor_ref[b, i : i + 1, :] * outer).astype(BF16)


def intra_kernel(plan, slot, first_part, table_ref, k_ref, v_ref, *refs):
    size, hpo, length = plan.size, plan.hpo, plan.length
    copies = None
    if first_part:
        q_hbm, cot_hbm = refs[:2]
        q_refs, cot_refs = refs[2 : 2 + size], refs[2 + size : 2 + 2 * size]
        mask_ref, out_ref, decayed_ref, probs_ref, weight_ref, sems = refs[2 + 2 * size :]
        q_ref = q_refs[slot]

        def loads(other):
            lanes = plan.lanes(other)
            return (
                pltpu.make_async_copy(q_hbm.at[:, lanes], q_refs[other], sems.at[0, other]),
                pltpu.make_async_copy(cot_hbm.at[:, lanes], cot_refs[other], sems.at[1, other]),
            )

        copies = [loads(other) for other in [slot] + [other for other in range(size) if other != slot]]
        others = [slot] + [other for other in range(size) if other != slot]
        for other, pair in zip(others, copies):

            @plan.guard(other)
            def _():
                for copy in pair:
                    copy.start()

        mask_ref[...] = block_mask(table_ref[0])
    else:
        q_ref, mask_ref, out_ref, decayed_ref, probs_ref, weight_ref = refs

    @plan.guard(slot)
    def _():
        if copies is not None:
            copies[0][0].wait()
        table = table_ref[slot]
        columns = table.T
        for i in range(hpo):
            lanes = plan.head(i)
            turned = q_ref[:, lanes].T
            decayed_ref[lanes, :] = (turned.astype(F32) * table[hpo + i : hpo + i + 1]).astype(BF16)
            outs = [None] * (length // HALF)
            at = 0
            for first in range(0, length, HALF):
                rows = slice(first, first + HALF)
                gap = table[i : i + 1, first:] - columns[rows, i : i + 1]
                weight = jnp.exp2(gap + mask_ref[rows, first:])
                probs = (dot(k_ref[rows, lanes], turned[:, first:]) * weight).astype(BF16)
                weight_ref[i, :, at : at + length - first] = weight.astype(BF16)
                probs_ref[i, :, at : at + length - first] = probs
                for j in range(first, length, HALF):
                    part = dot(probs[:, j - first : j - first + HALF], v_ref[rows, lanes], ((0,), (0,)))
                    outs[j // HALF] = part if outs[j // HALF] is None else outs[j // HALF] + part
                at += length - first
            for j, out in enumerate(outs):
                out_ref[j * HALF : (j + 1) * HALF, lanes] = out

    if copies is not None:
        for other, pair in zip(others, copies):

            @plan.guard(other)
            def _():
                for copy in pair if other != slot else pair[1:]:
                    copy.wait()


def token_rows(total):
    length = total.shape[0]
    return jnp.concatenate(
        [jnp.sum(total[i : i + 128].T, axis=0, keepdims=True) for i in range(0, length, 128)], axis=0
    )


def output_kernel(plan, slot, first_part, last_part, table_ref, q_ref, cot_ref, intra_ref, state_ref, *refs):
    hpo = plan.hpo
    if not first_part:
        old_ref, refs = refs[0], refs[1:]
    out_ref, total_ref = refs[:2]
    if first_part:
        total_ref[...] = jnp.zeros_like(total_ref)
    else:
        total_ref[...] = old_ref[...]

    @plan.guard(slot)
    def _():
        columns = table_ref[slot].T
        square, cross = total_ref[0], total_ref[1]
        for i in range(hpo):
            lanes = plan.head(i)
            carried = dot(q_ref[:, lanes], state_ref[lanes, :])
            out = intra_ref[:, lanes] + columns[:, hpo + i : hpo + i + 1] * carried
            out_ref[:, lanes] = out
            square = square + out * out
            cross = cross + cot_ref[:, lanes].astype(F32) * out
        total_ref[0] = square
        total_ref[1] = cross

    if last_part:
        refs[2][...] = jnp.concatenate([token_rows(total_ref[0]), token_rows(total_ref[1])], axis=0)


def factors(sums_refs, factor_ref):
    total = sums_refs[0][...]
    for ref in sums_refs[1:]:
        total = total + ref[...]
    lines = total.shape[0] // 2
    full = HEAD_TOTAL * HEAD_DIM
    scale = lax.rsqrt(total[:lines] / full + EPS)
    slope = scale * scale * scale * total[lines:] / full
    turned = jnp.concatenate([scale, slope], axis=0).T
    for j in range(2):
        for i in range(lines):
            column = turned[:, j * lines + i : j * lines + i + 1]
            factor_ref[j, i * 128 : (i + 1) * 128, :] = jnp.broadcast_to(column, (128, factor_ref.shape[2]))


def gout_kernel(plan, slot, count, *refs):
    if count:
        factor_ref = refs[count + 3]
        factors(refs[:count], factor_ref)
        out_ref, cot_ref, decayed_ref, _, gout_ref, sent_ref = refs[count:]
    else:
        factor_ref, out_ref, cot_ref, decayed_ref, gout_ref, sent_ref = refs

    @plan.guard(slot)
    def _():
        for i in range(plan.hpo):
            lanes = plan.head(i)
            gout = factor_ref[0] * cot_ref[:, lanes].astype(F32) - factor_ref[1] * out_ref[:, lanes]
            gout = gout.astype(BF16)
            gout_ref[:, lanes] = gout
            sent_ref[lanes, :] = dot(decayed_ref[lanes, :], gout).astype(BF16)


def attn_kernel(plan, factor_ref, *refs):
    size = plan.size
    for slot, (out_ref, attn_ref) in enumerate(zip(refs[:size], refs[size:])):

        @plan.guard(slot)
        def _():
            for i in range(plan.hpo):
                lanes = plan.head(i)
                attn_ref[:, lanes] = (factor_ref[0] * out_ref[:, lanes]).astype(BF16)


def stores(plan, slots, in_refs, hbms, sems):
    return [
        (slot, pltpu.make_async_copy(ref, hbm.at[:, plan.lanes(slot)], sems.at[n]))
        for n, (slot, ref, hbm) in enumerate(zip(slots, in_refs, hbms))
    ]


def start_all(plan, copies):
    for slot, copy in copies:
        plan.guard(slot)(copy.start)


def wait_all(plan, copies):
    for slot, copy in copies:
        plan.guard(slot)(copy.wait)


def gradient_kernel(plan, slot, finished, fresh, *refs):
    table_ref, k_ref, v_ref, q_ref, gout_ref, turned_ref, probs_ref, weight_ref, state_ref = refs[:9]
    refs = refs[9:]
    done_refs, refs = refs[: len(finished)], refs[len(finished) :]
    copies = []
    if finished:
        if not fresh:
            refs = refs[1:]
        copies = stores(plan, finished, done_refs, [refs[0]] * len(finished), refs[-1])
        refs = refs[1:-1]
    start_all(plan, copies)
    gq_ref, gk_ref, gv_ref = refs
    hpo, length = plan.hpo, plan.length

    @plan.guard(slot)
    def _():
        table = table_ref[slot]
        for i in range(hpo):
            lanes = plan.head(i)
            gout_turned = gout_ref[:, lanes].T
            totals = table[hpo + i : hpo + i + 1] * dot(state_ref[lanes, :], gout_turned)
            totals = [totals[:, j : j + HALF] for j in range(0, length, HALF)]
            at = 0
            for first in range(0, length, HALF):
                rows, later = slice(first, first + HALF), slice(first, length)
                size = length - first
                gv_ref[rows, lanes] = dot(probs_ref[i, :, at : at + size], gout_ref[later, lanes])
                grads = dot(v_ref[rows, lanes], gout_turned[:, later])
                grads = (grads * weight_ref[i, :, at : at + size].astype(F32)).astype(BF16)
                gk_ref[rows, lanes] = dot(grads, q_ref[later, lanes])
                piece = dot(turned_ref[lanes, rows], grads)
                for j in range(first, length, HALF):
                    totals[j // HALF] = totals[j // HALF] + piece[:, j - first : j - first + HALF]
                at += size
            for j, total in enumerate(totals):
                gq_ref[j * HALF : (j + 1) * HALF, lanes] = total.astype(BF16).T

    wait_all(plan, copies)


def final_kernel(plan, slot, finished, fresh, last_part, *refs):
    table_ref, k_ref, v_ref, gkp_ref, gvp_ref, back_ref = refs[:6]
    refs = refs[6:]
    done_refs, refs = refs[: len(finished)], refs[len(finished) :]
    if not all(fresh):
        refs = refs[fresh.count(False) :]
    gq_hbm, gk_hbm, gv_hbm, gk_ref, gv_ref, sems = refs
    hbm_of = {"gq": gq_hbm, "gk": gk_hbm, "gv": gv_hbm}
    copies = stores(plan, [s for _, s in finished], done_refs, [hbm_of[name] for name, _ in finished], sems)
    start_all(plan, copies)

    @plan.guard(slot)
    def _():
        columns = table_ref[slot].T
        for i in range(plan.hpo):
            lanes = plan.head(i)
            leave = columns[:, 2 * plan.hpo + i : 2 * plan.hpo + i + 1]
            back = back_ref[lanes, :]
            gk_ref[:, lanes] = (gkp_ref[:, lanes] + leave * dot_nt(v_ref[:, lanes], back)).astype(BF16)
            gv_ref[:, lanes] = (gvp_ref[:, lanes] + leave * dot(k_ref[:, lanes], back)).astype(BF16)

    if last_part:
        own = len(finished)
        lanes = plan.lanes(slot)
        tail = [
            (slot, pltpu.make_async_copy(gk_ref, gk_hbm.at[:, lanes], sems.at[own])),
            (slot, pltpu.make_async_copy(gv_ref, gv_hbm.at[:, lanes], sems.at[own + 1])),
        ]
        start_all(plan, tail)
        copies = copies + tail
    wait_all(plan, copies)


def exchange(arrays, size, halves, target):
    def pairs(slot):
        return [(base + i, base + target(i, slot, size)) for base in range(0, halves * size, size) for i in range(size)]

    return [arrays[0]] + [lax.ppermute(arrays[slot], "seq", pairs(slot)) for slot in range(1, size)]


def per_device(queries, keys, values, cotangent, log_decay, starts):
    length, width = queries.shape
    heads = log_decay.shape[0]
    dim = width // heads
    blocks = lax.axis_size("seq")
    shares = lax.axis_size("head")
    halves = 2 if blocks % 2 == 0 else 1
    size = blocks // halves
    plan = Plan(heads, dim, length, size)
    hpo, span = plan.hpo, plan.span
    params = pltpu.CompilerParams(vmem_limit_bytes=12 << 20)

    inside = pl.BlockSpec(memory_space=pltpu.VMEM)
    unused = pl.BlockSpec(memory_space=pl.ANY)
    hbm = pl.BlockSpec(memory_space=pltpu.HBM)
    dma = pltpu.SemaphoreType.DMA
    whole = pltpu.HBM((length, width), BF16)

    def outside(array):
        return pltpu.with_memory_space_constraint(array, pltpu.HBM)

    def held(dtype, columns=span):
        return pltpu.VMEM((length, columns), dtype)

    def cost(products, exps=0):
        return pl.CostEstimate(flops=2 * hpo * products, bytes_accessed=length * span, transcendentals=hpo * exps)

    def call(kernel, name, operands, results, work, extra=(), scratch=(), aliases=None):
        far = [isinstance(a, tuple) for a in operands]
        return pl.pallas_call(
            kernel,
            in_specs=[hbm if f else inside for f in far] + [unused] * len(extra),
            out_specs=[hbm if r is whole else inside for r in results],
            out_shape=list(results),
            scratch_shapes=list(scratch),
            input_output_aliases=aliases or {},
            compiler_params=params,
            cost_estimate=work,
            name=name,
        )(*[a[0] if f else a for a, f in zip(operands, far)], *extra)

    def scan(arrays, carries, after, later):
        forward = carries is None
        factor = pltpu.VMEM((size, 8, dim), F32)
        local, total, factor, *rest = call(
            functools.partial(scan_kernel, plan, forward),
            "scan",
            [*arrays] + ([] if forward else [carries]),
            [pltpu.VMEM((size, span, dim), F32), pltpu.VMEM((span, dim), BF16), factor] + ([factor] if forward else []),
            None,
            after,
            [pltpu.VMEM((size, *arrays[0].shape), BF16)],
        )
        if halves == 2:
            pairs = [(i, i + size) if forward else (i + size, i) for i in range(size)]
            outer = lax.ppermute(total, "seq", pairs)
        else:
            outer = jnp.zeros_like(total)
        back = call(
            functools.partial(return_kernel, plan),
            "return",
            [local, factor, outer],
            [pltpu.VMEM((span, dim), BF16)] * size,
            None,
            later,
        )
        return exchange(back, size, halves, inverse), (rest[0] if forward else None)

    big, small = length * length * dim, length * dim * dim
    queries, keys, values, cotangent = (outside(a) for a in (queries, keys, values, cotangent))
    results = call(
        functools.partial(update_kernel, plan),
        "update",
        [(outside(log_decay),), (outside(starts.reshape(1, length)),), (keys,), (values,)],
        [pltpu.VMEM((span + ROWS, dim), BF16)] * size
        + [held(BF16)] * (2 * size)
        + [pltpu.VMEM((span, length), BF16)] * size
        + [pltpu.VMEM((size, ROWS, length), F32)],
        cost(size * small),
        scratch=[
            pltpu.VMEM((heads, length), F32),
            pltpu.VMEM((1, length), jnp.int32),
            pltpu.VMEM((heads // hpo, ROWS, length), F32),
            dma((2,)),
            dma((2, size)),
        ],
    )
    sent, k, v, turned = (results[i * size : (i + 1) * size] for i in range(4))
    table = results[-1]
    received = exchange(sent, size, halves, partner)

    lower = length * (length + HALF) // 2 // HALF
    kept = pltpu.VMEM((hpo, HALF, lower), BF16)
    intra, decayed, probs, weights = [], [], [], []
    for slot in range(size):
        first = slot == 0
        results = call(
            functools.partial(intra_kernel, plan, slot, first),
            "intra",
            [table, k[slot], v[slot]] + ([(queries,), (cotangent,)] if first else [q[slot], mask]),
            ([held(BF16)] * (2 * size) + [pltpu.VMEM((length, length), F32)] if first else [])
            + [held(F32), pltpu.VMEM((span, length), BF16), kept, kept],
            cost(2 * big, length * length),
            scratch=[dma((2, size))] if first else [],
        )
        if first:
            q, cot, mask = results[:size], results[size : 2 * size], results[2 * size]
        for kind, result in zip((intra, decayed, probs, weights), results[-4:]):
            kind.append(result)

    middle = -(-size // 2)
    received, carries = scan(received, None, intra[:middle], intra[middle:])

    outputs = []
    total = sums = None
    for slot in range(size):
        first, last = slot == 0, slot == size - 1
        out, total, *rest = call(
            functools.partial(output_kernel, plan, slot, first, last),
            "output",
            [table, q[slot], cot[slot], intra[slot], received[slot]] + ([] if first else [total]),
            [held(F32), pltpu.VMEM((2, length, dim), F32)] + ([pltpu.VMEM((2 * length // 128, 128), F32)] if last else []),
            cost(small),
        )
        outputs.append(out)
        sums = rest[0] if last else sums
    states = received

    everyone = [sums] + [
        lax.ppermute(sums, "head", [(i, (i + k) % shares) for i in range(shares)]) for k in range(1, shares)
    ]

    gout, sent = [None] * size, [None] * size
    factor = None
    for slot in order(size):
        first = factor is None
        *rest, gout[slot], sent[slot] = call(
            functools.partial(gout_kernel, plan, slot, shares if first else 0),
            "gout",
            (everyone if first else [factor]) + [outputs[slot], cot[slot], decayed[slot]],
            ([pltpu.VMEM((2, length, dim), F32)] if first else []) + [held(BF16), pltpu.VMEM((span, dim), BF16)],
            cost(small),
        )
        factor = rest[0] if first else factor
    received = exchange(sent, size, halves, partner)
    attn = call(
        functools.partial(attn_kernel, plan),
        "attn",
        [factor, *outputs],
        [held(BF16)] * size,
        cost(small),
    )

    gq, gk_part, gv_part = [], [], []
    attn_whole = gq_whole = None
    for slot in range(size):
        fresh = slot < 2
        finished = list(range(size)) if slot == 0 else [slot - 1]
        done = list(attn) if slot == 0 else [gq[slot - 1]]
        operands = [table, k[slot], v[slot], q[slot], gout[slot], turned[slot], probs[slot], weights[slot], states[slot]]
        operands += done
        results = call(
            functools.partial(gradient_kernel, plan, slot, finished, fresh),
            "gradient",
            operands + ([] if fresh else [(gq_whole,)]),
            [whole, held(BF16), held(F32), held(F32)],
            cost(4 * big),
            scratch=[dma((len(finished),))],
            aliases={} if fresh else {len(operands): 0},
        )
        if slot == 0:
            attn_whole = results[0]
        else:
            gq_whole = results[0]
        for kind, result in zip((gq, gk_part, gv_part), results[1:]):
            kind.append(result)

    received, _ = scan(received, carries, gk_part[:1], gk_part[1:-1])

    gk_whole = gv_whole = None
    gk = gv = None
    for slot in range(size):
        first, last = slot == 0, slot == size - 1
        finished = [("gq", size - 1)] if first else [("gk", slot - 1), ("gv", slot - 1)]
        done = [gq[-1]] if first else [gk, gv]
        operands = [table, k[slot], v[slot], gk_part[slot], gv_part[slot], received[slot]] + done
        held_back = [gq_whole, gk_whole, gv_whole]
        fresh = [a is None for a in held_back]
        aliases = {}
        chained = []
        for n, array in enumerate(held_back):
            if array is not None:
                aliases[len(operands) + len(chained)] = n
                chained.append((array,))
        gq_whole, gk_whole, gv_whole, gk, gv = call(
            functools.partial(final_kernel, plan, slot, finished, fresh, last),
            "final",
            operands + chained,
            [whole] * 3 + [held(BF16)] * 2,
            cost(2 * small),
            scratch=[dma((len(finished) + 2,))],
            aliases=aliases,
        )
    return (attn_whole, gq_whole, gk_whole, gv_whole)


def solution(mesh):
    wide = P("seq", "head")
    return jax.shard_map(
        per_device,
        mesh=mesh,
        in_specs=(wide, wide, wide, wide, P("head", "seq"), P("seq")),
        out_specs=(wide, wide, wide, wide),
        check_vma=False,
    )
```

```python
import functools

import jax
import jax.numpy as jnp
from jax import lax
from jax.experimental import pallas as pl
from jax.experimental.pallas import tpu as pltpu
from jax.sharding import PartitionSpec as P

HEAD_TOTAL = 64
HEAD_DIM = 128
EPS = 1e-05
LOG2E = 1.4426950408889634
MASKED = -1e30
ROWS = 16
HALF = 256
F32 = jnp.float32
BF16 = jnp.bfloat16


def dot(a, b, dims=((1,), (0,))):
    return lax.dot_general(a, b, (dims, ((), ())), preferred_element_type=F32)


def dot_nt(a, b):
    return dot(a, b, ((1,), (1,)))


def three_parts(x):
    high = x.astype(BF16).astype(F32)
    rest = x - high
    middle = rest.astype(BF16).astype(F32)
    return high, middle, rest - middle


def lanes_of(index, size):
    return pl.ds(index * size if isinstance(index, int) else pl.multiple_of(index * size, size), size)


def partner(place, slot, size):
    if size & (size - 1):
        return (place + slot) % size
    return place ^ (3 - slot if slot in (1, 2) and size > 2 else slot)


def inverse(place, slot, size):
    return partner(place, slot, size) if size & (size - 1) == 0 else (place + size - slot) % size


def my_place(size):
    return lax.rem(lax.axis_index("seq"), size)


def ones_where(keep):
    return jnp.where(keep, 1.0, 0.0).astype(BF16)


def running_sum(x, upper):
    rows = x.shape[0]
    parts = jnp.concatenate(three_parts(x), axis=0).astype(BF16)
    sums = dot(parts, upper)
    return sums[:rows] + sums[rows : 2 * rows] + sums[2 * rows :]


def diagonal(blocks):
    if len(blocks) == 1:
        return blocks[0]
    zero = jnp.zeros_like(blocks[0])
    rows = [[block if i == j else zero for j in range(len(blocks))] for i, block in enumerate(blocks)]
    return jnp.concatenate([jnp.concatenate(row, axis=1) for row in rows], axis=0)


def block_mask(table):
    length = table.shape[1]
    row = table[ROWS - 1 :, :]
    column = table.T[:, ROWS - 1 :]
    down = lax.broadcasted_iota(jnp.int32, (length, length), 0)
    across = lax.broadcasted_iota(jnp.int32, (length, length), 1)
    return jnp.where((across >= down) & (row == column), 0.0, MASKED)


class Plan:
    def __init__(self, heads, dim, length, size):
        self.heads, self.dim, self.length, self.size = heads, dim, length, size
        self.hpo = -(-heads // size)
        self.span = self.hpo * dim

    def lanes(self, slot):
        start = partner(my_place(self.size), slot, self.size) * self.span
        return pl.ds(pl.multiple_of(start, self.span), self.span)

    def head(self, i):
        return slice(i * self.dim, (i + 1) * self.dim)

    def tiles(self):
        for j in range(self.length // HALF):
            start = HALF * (j * (j + 1) // 2)
            yield slice(j * HALF, (j + 1) * HALF), slice(0, (j + 1) * HALF), slice(start, start + (j + 1) * HALF)

    def pairs(self):
        step = 2 if self.hpo % 2 == 0 else 1
        return [list(range(i, i + step)) for i in range(0, self.hpo, step)]

    def columns(self, pair):
        return slice(pair[0] * self.dim, (pair[-1] + 1) * self.dim)

    def guard(self, slot):
        return pl.when(partner(my_place(self.size), slot, self.size) * self.hpo < self.heads)


def order(size):
    return list(range(1, size)) + [0]


def update_kernel(plan, logs_hbm, starts_hbm, k_hbm, v_hbm, *refs):
    size, hpo, dim, heads = plan.size, plan.hpo, plan.dim, plan.heads
    sent_refs, k_refs, v_refs, turned_refs = (refs[i * size : (i + 1) * size] for i in range(4))
    table_ref, logs_ref, starts_ref, natural_ref, small_sems, sems = refs[4 * size :]
    length = plan.length
    copies = [
        pltpu.make_async_copy(logs_hbm, logs_ref, small_sems.at[0]),
        pltpu.make_async_copy(starts_hbm, starts_ref, small_sems.at[1]),
    ]
    for copy in copies:
        copy.start()

    def loads(slot):
        lanes = plan.lanes(slot)
        return (
            pltpu.make_async_copy(k_hbm.at[:, lanes], k_refs[slot], sems.at[0, slot]),
            pltpu.make_async_copy(v_hbm.at[:, lanes], v_refs[slot], sems.at[1, slot]),
        )

    for slot in order(size):

        @plan.guard(slot)
        def _():
            for copy in loads(slot):
                copy.start()

    down = lax.broadcasted_iota(jnp.int32, (length, length), 0)
    across = lax.broadcasted_iota(jnp.int32, (length, length), 1)
    upper = ones_where(down <= across)
    for copy in copies:
        copy.wait()
    flags = jnp.broadcast_to(starts_ref[...].astype(F32), (8, length))
    sums = running_sum(jnp.concatenate([logs_ref[...], flags], axis=0), upper)
    logs, count = sums[:heads] * LOG2E, sums[heads : heads + 1]
    last = slice(length - 1, length)
    enter = jnp.where(count == 0.0, jnp.exp2(logs), 0.0)
    leave = jnp.where(count == count[:, last], jnp.exp2(logs[:, last] - logs), 0.0)
    fill = jnp.broadcast_to(count, (ROWS - 3 * hpo, length))
    for owner in range(heads // hpo):
        rows = slice(owner * hpo, (owner + 1) * hpo)
        natural_ref[owner] = jnp.concatenate([logs[rows], enter[rows], leave[rows], fill], axis=0)
    line = lax.broadcasted_iota(jnp.int32, (ROWS, dim), 0)

    for slot in order(size):

        @plan.guard(slot)
        def _():
            table = natural_ref[partner(my_place(size), slot, size)]
            table_ref[slot] = table
            for copy in loads(slot):
                copy.wait()
            tile = jnp.zeros((ROWS, dim), F32)
            for i in range(hpo):
                lanes = plan.head(i)
                turned = k_refs[slot][:, lanes].T
                turned_refs[slot][lanes, :] = turned
                decayed = (turned.astype(F32) * table[2 * hpo + i : 2 * hpo + i + 1]).astype(BF16)
                sent_refs[slot][lanes, :] = dot(decayed, v_refs[slot][:, lanes]).astype(BF16)
                carry = jnp.broadcast_to(table[hpo + i : hpo + i + 1, last], (ROWS, dim))
                for j, part in enumerate(three_parts(carry)):
                    tile = jnp.where(line == 3 * i + j, part, tile)
            sent_refs[slot][hpo * dim :, :] = tile.astype(BF16)


def scan_kernel(plan, forward, *refs):
    size, hpo, dim = plan.size, plan.hpo, plan.dim
    in_refs, refs = refs[:size], refs[size:]
    if forward:
        local_ref, total_ref, factor_ref, carry_ref, ordered_ref = refs[-5:]
    else:
        carry_ref = refs[0]
        local_ref, total_ref, factor_ref, ordered_ref = refs[-4:]
    me = my_place(size)
    for slot, in_ref in enumerate(in_refs):
        ordered_ref[inverse(me, slot, size)] = in_ref[...]
    if forward:
        for b in range(size):
            tile = ordered_ref[b, hpo * dim :, :].astype(F32)
            for i in range(hpo):
                carry_ref[b, i : i + 1, :] = tile[3 * i : 3 * i + 1] + tile[3 * i + 1 : 3 * i + 2] + tile[3 * i + 2 : 3 * i + 3]
    for i in range(hpo):
        rows = plan.head(i)
        state = jnp.zeros((dim, dim), F32)
        factor = jnp.ones((1, dim), F32)
        for b in range(size) if forward else reversed(range(size)):
            carry = carry_ref[b, i : i + 1, :]
            local_ref[b, rows, :] = state
            factor_ref[b, i : i + 1, :] = factor
            state = carry * state + ordered_ref[b, rows, :].astype(F32)
            factor = factor * carry
        total_ref[rows, :] = state.astype(BF16)


def return_kernel(plan, forward, local_ref, factor_ref, outer_ref, *refs):
    out_refs = refs[-plan.size :]
    me = my_place(plan.size)
    upper = lax.axis_index("seq") >= plan.size
    takes = upper if forward else jnp.logical_not(upper)
    for i in range(plan.hpo):
        rows = plan.head(i)
        outer = jnp.where(takes, outer_ref[rows, :].astype(F32), 0.0)
        for slot, out_ref in enumerate(out_refs):
            b = inverse(me, slot, plan.size)
            out_ref[rows, :] = (local_ref[b, rows, :] + factor_ref[b, i : i + 1, :] * outer).astype(BF16)


def intra_kernel(plan, slot, first_part, table_ref, k_ref, v_ref, *refs):
    size, hpo, length = plan.size, plan.hpo, plan.length
    copies = None
    if first_part:
        q_hbm, cot_hbm = refs[:2]
        q_refs, cot_refs = refs[2 : 2 + size], refs[2 + size : 2 + 2 * size]
        mask_ref, out_ref, decayed_ref, probs_ref, weight_ref, sems = refs[2 + 2 * size :]
        q_ref = q_refs[slot]

        def loads(other):
            lanes = plan.lanes(other)
            return (
                pltpu.make_async_copy(q_hbm.at[:, lanes], q_refs[other], sems.at[0, other]),
                pltpu.make_async_copy(cot_hbm.at[:, lanes], cot_refs[other], sems.at[1, other]),
            )

        copies = [loads(other) for other in [slot] + [other for other in range(size) if other != slot]]
        others = [slot] + [other for other in range(size) if other != slot]
        for other, pair in zip(others, copies):

            @plan.guard(other)
            def _():
                for copy in pair:
                    copy.start()

        mask_ref[...] = block_mask(table_ref[0])
    else:
        q_ref, mask_ref, out_ref, decayed_ref, probs_ref, weight_ref = refs

    @plan.guard(slot)
    def _():
        if copies is not None:
            copies[0][0].wait()
        table = table_ref[slot]
        columns = table.T
        for i in range(hpo):
            lanes = plan.head(i)
            turned = q_ref[:, lanes].T
            decayed_ref[lanes, :] = (turned.astype(F32) * table[hpo + i : hpo + i + 1]).astype(BF16)
            for later, seen, kept in plan.tiles():
                gap = table[i : i + 1, later] - columns[seen, i : i + 1]
                weight = jnp.exp2(gap + mask_ref[seen, later])
                probs = (dot(k_ref[seen, lanes], turned[:, later]) * weight).astype(BF16)
                weight_ref[i, kept, :] = weight.astype(BF16)
                probs_ref[i, kept, :] = probs
                out_ref[later, lanes] = dot(probs, v_ref[seen, lanes], ((0,), (0,)))

    if copies is not None:
        for other, pair in zip(others, copies):

            @plan.guard(other)
            def _():
                for copy in pair if other != slot else pair[1:]:
                    copy.wait()


def token_rows(total):
    ones = jnp.ones((ROWS, total.shape[1]), BF16)
    row = sum(dot_nt(ones, part.astype(BF16)) for part in three_parts(total))[:1]
    return jnp.concatenate([row[:, i : i + 128] for i in range(0, total.shape[0], 128)], axis=0)


def output_kernel(plan, slot, first_part, last_part, table_ref, q_ref, cot_ref, intra_ref, state_ref, *refs):
    hpo = plan.hpo
    if not first_part:
        old_ref, refs = refs[0], refs[1:]
    out_ref, total_ref = refs[:2]
    if first_part:
        total_ref[...] = jnp.zeros_like(total_ref)
    else:
        total_ref[...] = old_ref[...]

    @plan.guard(slot)
    def _():
        columns = table_ref[slot].T
        square, cross = total_ref[0], total_ref[1]
        for pair in plan.pairs():
            states = diagonal([state_ref[plan.head(i), :] for i in pair])
            both = dot(q_ref[:, plan.columns(pair)], states)
            for j, i in enumerate(pair):
                lanes = plan.head(i)
                out = intra_ref[:, lanes] + columns[:, hpo + i : hpo + i + 1] * both[:, plan.head(j)]
                out_ref[:, lanes] = out
                square = square + out * out
                cross = cross + cot_ref[:, lanes].astype(F32) * out
        total_ref[0] = square
        total_ref[1] = cross

    if last_part:
        refs[2][...] = jnp.concatenate([token_rows(total_ref[0]), token_rows(total_ref[1])], axis=0)


def factors(sums_refs, factor_ref):
    total = sums_refs[0][...]
    for ref in sums_refs[1:]:
        total = total + ref[...]
    lines = total.shape[0] // 2
    full = HEAD_TOTAL * HEAD_DIM
    scale = lax.rsqrt(total[:lines] / full + EPS)
    slope = scale * scale * scale * total[lines:] / full
    turned = jnp.concatenate([scale, slope], axis=0).T
    for j in range(2):
        for i in range(lines):
            column = turned[:, j * lines + i : j * lines + i + 1]
            factor_ref[j, i * 128 : (i + 1) * 128, :] = jnp.broadcast_to(column, (128, factor_ref.shape[2]))


def gout_kernel(plan, slot, count, *refs):
    if count:
        factor_ref = refs[count + 3]
        factors(refs[:count], factor_ref)
        out_ref, cot_ref, decayed_ref, _, gout_ref, sent_ref = refs[count:]
    else:
        factor_ref, out_ref, cot_ref, decayed_ref, gout_ref, sent_ref = refs

    @plan.guard(slot)
    def _():
        for i in range(plan.hpo):
            lanes = plan.head(i)
            gout = factor_ref[0] * cot_ref[:, lanes].astype(F32) - factor_ref[1] * out_ref[:, lanes]
            gout = gout.astype(BF16)
            gout_ref[:, lanes] = gout
            sent_ref[lanes, :] = dot(decayed_ref[lanes, :], gout).astype(BF16)


def attn_kernel(plan, factor_ref, *refs):
    size = plan.size
    for slot, (out_ref, attn_ref) in enumerate(zip(refs[:size], refs[size:])):

        @plan.guard(slot)
        def _():
            for i in range(plan.hpo):
                lanes = plan.head(i)
                attn_ref[:, lanes] = (factor_ref[0] * out_ref[:, lanes]).astype(BF16)


def stores(plan, slots, in_refs, hbms, sems):
    return [
        (slot, pltpu.make_async_copy(ref, hbm.at[:, plan.lanes(slot)], sems.at[n]))
        for n, (slot, ref, hbm) in enumerate(zip(slots, in_refs, hbms))
    ]


def start_all(plan, copies):
    for slot, copy in copies:
        plan.guard(slot)(copy.start)


def wait_all(plan, copies):
    for slot, copy in copies:
        plan.guard(slot)(copy.wait)


def gradient_kernel(plan, slot, finished, fresh, *refs):
    table_ref, k_ref, v_ref, q_ref, gout_ref, turned_ref, probs_ref, weight_ref, state_ref = refs[:9]
    refs = refs[9:]
    done_refs, refs = refs[: len(finished)], refs[len(finished) :]
    copies = []
    if finished:
        if not fresh:
            refs = refs[1:]
        copies = stores(plan, finished, done_refs, [refs[0]] * len(finished), refs[-1])
        refs = refs[1:-1]
    start_all(plan, copies)
    gq_ref, gk_ref, gv_ref = refs
    hpo, length = plan.hpo, plan.length

    @plan.guard(slot)
    def _():
        table = table_ref[slot]
        for i in range(hpo):
            lanes = plan.head(i)
            gout_turned = gout_ref[:, lanes].T
            carried = table[hpo + i : hpo + i + 1] * dot(state_ref[lanes, :], gout_turned)
            for later, seen, kept in reversed(list(plan.tiles())):
                grads = dot(v_ref[seen, lanes], gout_turned[:, later])
                grads = (grads * weight_ref[i, kept, :].astype(F32)).astype(BF16)
                from_probs = dot(probs_ref[i, kept, :], gout_ref[later, lanes])
                from_grads = dot(grads, q_ref[later, lanes])
                if seen.stop == length:
                    gv_ref[:, lanes] = from_probs
                    gk_ref[:, lanes] = from_grads
                else:
                    gv_ref[seen, lanes] += from_probs
                    gk_ref[seen, lanes] += from_grads
                total = carried[:, later] + dot(turned_ref[lanes, seen], grads)
                gq_ref[later, lanes] = total.astype(BF16).T

    wait_all(plan, copies)


def final_kernel(plan, slot, finished, fresh, last_part, *refs):
    table_ref, k_ref, v_ref, gkp_ref, gvp_ref, back_ref = refs[:6]
    refs = refs[6:]
    done_refs, refs = refs[: len(finished)], refs[len(finished) :]
    if not all(fresh):
        refs = refs[fresh.count(False) :]
    gq_hbm, gk_hbm, gv_hbm, gk_ref, gv_ref, sems = refs
    hbm_of = {"gq": gq_hbm, "gk": gk_hbm, "gv": gv_hbm}
    copies = stores(plan, [s for _, s in finished], done_refs, [hbm_of[name] for name, _ in finished], sems)
    start_all(plan, copies)

    tails = []
    if last_part:
        for n, pair in enumerate(plan.pairs()):
            for m, (ref, target) in enumerate(((gk_ref, gk_hbm), (gv_ref, gv_hbm))):
                start = partner(my_place(plan.size), slot, plan.size) * plan.span
                width = len(pair) * plan.dim
                lanes = pl.ds(pl.multiple_of(start + n * width, width), width)
                sem = sems.at[len(finished) + 2 * n + m]
                tails.append((slot, pltpu.make_async_copy(ref.at[:, plan.columns(pair)], target.at[:, lanes], sem)))

    @plan.guard(slot)
    def _():
        columns = table_ref[slot].T
        for n, pair in enumerate(plan.pairs()):
            back = diagonal([back_ref[plan.head(i), :] for i in pair])
            both = plan.columns(pair)
            from_values = dot_nt(v_ref[:, both], back)
            from_keys = dot(k_ref[:, both], back)
            for j, i in enumerate(pair):
                lanes, part = plan.head(i), plan.head(j)
                leave = columns[:, 2 * plan.hpo + i : 2 * plan.hpo + i + 1]
                gk_ref[:, lanes] = (gkp_ref[:, lanes] + leave * from_values[:, part]).astype(BF16)
                gv_ref[:, lanes] = (gvp_ref[:, lanes] + leave * from_keys[:, part]).astype(BF16)
            for _, copy in tails[2 * n : 2 * n + 2]:
                copy.start()

    wait_all(plan, copies + tails)


def exchange(arrays, size, halves, target):
    def pairs(slot):
        return [(base + i, base + target(i, slot, size)) for base in range(0, halves * size, size) for i in range(size)]

    return [arrays[0]] + [lax.ppermute(arrays[slot], "seq", pairs(slot)) for slot in range(1, size)]


def per_device(queries, keys, values, cotangent, log_decay, starts):
    length, width = queries.shape
    heads = log_decay.shape[0]
    dim = width // heads
    blocks = lax.axis_size("seq")
    shares = lax.axis_size("head")
    halves = 2 if blocks % 2 == 0 else 1
    size = blocks // halves
    plan = Plan(heads, dim, length, size)
    hpo, span = plan.hpo, plan.span
    params = pltpu.CompilerParams(vmem_limit_bytes=12 << 20)

    inside = pl.BlockSpec(memory_space=pltpu.VMEM)
    unused = pl.BlockSpec(memory_space=pl.ANY)
    hbm = pl.BlockSpec(memory_space=pltpu.HBM)
    dma = pltpu.SemaphoreType.DMA
    whole = pltpu.HBM((length, width), BF16)

    def outside(array):
        return pltpu.with_memory_space_constraint(array, pltpu.HBM)

    def held(dtype, columns=span):
        return pltpu.VMEM((length, columns), dtype)

    def cost(products, exps=0):
        return pl.CostEstimate(flops=2 * hpo * products, bytes_accessed=length * span, transcendentals=hpo * exps)

    def call(kernel, name, operands, results, work, extra=(), scratch=(), aliases=None):
        far = [isinstance(a, tuple) for a in operands]
        return pl.pallas_call(
            kernel,
            in_specs=[hbm if f else inside for f in far] + [unused] * len(extra),
            out_specs=[hbm if r is whole else inside for r in results],
            out_shape=list(results),
            scratch_shapes=list(scratch),
            input_output_aliases=aliases or {},
            compiler_params=params,
            cost_estimate=work,
            name=name,
        )(*[a[0] if f else a for a, f in zip(operands, far)], *extra)

    def scan(arrays, carries, after, later):
        forward = carries is None
        factor = pltpu.VMEM((size, 8, dim), F32)
        local, total, factor, *rest = call(
            functools.partial(scan_kernel, plan, forward),
            "scan",
            [*arrays] + ([] if forward else [carries]),
            [pltpu.VMEM((size, span, dim), F32), pltpu.VMEM((span, dim), BF16), factor] + ([factor] if forward else []),
            None,
            after,
            [pltpu.VMEM((size, *arrays[0].shape), BF16)],
        )
        if halves == 2:
            pairs = [(i, (i + size) % (2 * size)) for i in range(2 * size)]
            outer = lax.ppermute(total, "seq", pairs)
        else:
            outer = jnp.zeros_like(total)
        back = call(
            functools.partial(return_kernel, plan, forward),
            "return",
            [local, factor, outer],
            [pltpu.VMEM((span, dim), BF16)] * size,
            None,
            later,
        )
        return exchange(back, size, halves, inverse), (rest[0] if forward else None)

    big, small = length * length * dim, length * dim * dim
    queries, keys, values, cotangent = (outside(a) for a in (queries, keys, values, cotangent))
    results = call(
        functools.partial(update_kernel, plan),
        "update",
        [(outside(log_decay),), (outside(starts.reshape(1, length)),), (keys,), (values,)],
        [pltpu.VMEM((span + ROWS, dim), BF16)] * size
        + [held(BF16)] * (2 * size)
        + [pltpu.VMEM((span, length), BF16)] * size
        + [pltpu.VMEM((size, ROWS, length), F32)],
        cost(size * small),
        scratch=[
            pltpu.VMEM((heads, length), F32),
            pltpu.VMEM((1, length), jnp.int32),
            pltpu.VMEM((heads // hpo, ROWS, length), F32),
            dma((2,)),
            dma((2, size)),
        ],
    )
    sent, k, v, turned = (results[i * size : (i + 1) * size] for i in range(4))
    table = results[-1]
    received = exchange(sent, size, halves, partner)

    kept = pltpu.VMEM((hpo, length * (length + HALF) // 2 // HALF, HALF), BF16)
    intra, decayed, probs, weights = [], [], [], []
    for slot in range(size):
        first = slot == 0
        results = call(
            functools.partial(intra_kernel, plan, slot, first),
            "intra",
            [table, k[slot], v[slot]] + ([(queries,), (cotangent,)] if first else [q[slot], mask]),
            ([held(BF16)] * (2 * size) + [pltpu.VMEM((length, length), F32)] if first else [])
            + [held(F32), pltpu.VMEM((span, length), BF16), kept, kept],
            cost(2 * big, length * length),
            scratch=[dma((2, size))] if first else [],
        )
        if first:
            q, cot, mask = results[:size], results[size : 2 * size], results[2 * size]
        for kind, result in zip((intra, decayed, probs, weights), results[-4:]):
            kind.append(result)

    middle = -(-size // 2)
    received, carries = scan(received, None, intra[:middle], intra[middle:])

    outputs = []
    total = sums = None
    for slot in range(size):
        first, last = slot == 0, slot == size - 1
        out, total, *rest = call(
            functools.partial(output_kernel, plan, slot, first, last),
            "output",
            [table, q[slot], cot[slot], intra[slot], received[slot]] + ([] if first else [total]),
            [held(F32), pltpu.VMEM((2, length, dim), F32)] + ([pltpu.VMEM((2 * length // 128, 128), F32)] if last else []),
            cost(small),
        )
        outputs.append(out)
        sums = rest[0] if last else sums
    states = received

    everyone = [sums] + [
        lax.ppermute(sums, "head", [(i, partner(i, k, shares)) for i in range(shares)]) for k in range(1, shares)
    ]

    gout, sent = [None] * size, [None] * size
    factor = None
    for slot in order(size):
        first = factor is None
        *rest, gout[slot], sent[slot] = call(
            functools.partial(gout_kernel, plan, slot, shares if first else 0),
            "gout",
            (everyone if first else [factor]) + [outputs[slot], cot[slot], decayed[slot]],
            ([pltpu.VMEM((2, length, dim), F32)] if first else []) + [held(BF16), pltpu.VMEM((span, dim), BF16)],
            cost(small),
        )
        factor = rest[0] if first else factor
    received = exchange(sent, size, halves, partner)
    attn = call(
        functools.partial(attn_kernel, plan),
        "attn",
        [factor, *outputs],
        [held(BF16)] * size,
        cost(small),
    )

    gq, gk_part, gv_part = [], [], []
    attn_whole = gq_whole = None
    for slot in range(size):
        fresh = slot < 2
        finished = list(range(size)) if slot == 0 else [slot - 1]
        done = list(attn) if slot == 0 else [gq[slot - 1]]
        operands = [table, k[slot], v[slot], q[slot], gout[slot], turned[slot], probs[slot], weights[slot], states[slot]]
        operands += done
        results = call(
            functools.partial(gradient_kernel, plan, slot, finished, fresh),
            "gradient",
            operands + ([] if fresh else [(gq_whole,)]),
            [whole, held(BF16), held(F32), held(F32)],
            cost(4 * big),
            scratch=[dma((len(finished),))],
            aliases={} if fresh else {len(operands): 0},
        )
        if slot == 0:
            attn_whole = results[0]
        else:
            gq_whole = results[0]
        for kind, result in zip((gq, gk_part, gv_part), results[1:]):
            kind.append(result)

    received, _ = scan(received, carries, gk_part[:1], gk_part[1:-1])

    gk_whole = gv_whole = None
    gk = gv = None
    for slot in range(size):
        first, last = slot == 0, slot == size - 1
        finished = [("gq", size - 1)] if first else [("gk", slot - 1), ("gv", slot - 1)]
        done = [gq[-1]] if first else [gk, gv]
        operands = [table, k[slot], v[slot], gk_part[slot], gv_part[slot], received[slot]] + done
        held_back = [gq_whole, gk_whole, gv_whole]
        fresh = [a is None for a in held_back]
        aliases = {}
        chained = []
        for n, array in enumerate(held_back):
            if array is not None:
                aliases[len(operands) + len(chained)] = n
                chained.append((array,))
        gq_whole, gk_whole, gv_whole, gk, gv = call(
            functools.partial(final_kernel, plan, slot, finished, fresh, last),
            "final",
            operands + chained,
            [whole] * 3 + [held(BF16)] * 2,
            cost(2 * small),
            scratch=[dma((len(finished) + 2 * len(plan.pairs()),))],
            aliases=aliases,
        )
    return (attn_whole, gq_whole, gk_whole, gv_whole)


def solution(mesh):
    wide = P("seq", "head")
    return jax.shard_map(
        per_device,
        mesh=mesh,
        in_specs=(wide, wide, wide, wide, P("head", "seq"), P("seq")),
        out_specs=(wide, wide, wide, wide),
        check_vma=False,
    )
```

```python
import functools

import jax
import jax.numpy as jnp
from jax import lax
from jax.experimental import pallas as pl
from jax.experimental.pallas import tpu as pltpu
from jax.sharding import PartitionSpec as P

HEAD_TOTAL = 64
HEAD_DIM = 128
EPS = 1e-05
LOG2E = 1.4426950408889634
MASKED = -1e30
ROWS = 16
HALF = 256
F32 = jnp.float32
BF16 = jnp.bfloat16


def dot(a, b, dims=((1,), (0,))):
    return lax.dot_general(a, b, (dims, ((), ())), preferred_element_type=F32)


def dot_nt(a, b):
    return dot(a, b, ((1,), (1,)))


def three_parts(x):
    high = x.astype(BF16).astype(F32)
    rest = x - high
    middle = rest.astype(BF16).astype(F32)
    return high, middle, rest - middle


def lanes_of(index, size):
    return pl.ds(index * size if isinstance(index, int) else pl.multiple_of(index * size, size), size)


def partner(place, slot, size):
    if size & (size - 1):
        return (place + slot) % size
    return place ^ (3 - slot if slot in (1, 2) and size > 2 else slot)


def inverse(place, slot, size):
    return partner(place, slot, size) if size & (size - 1) == 0 else (place + size - slot) % size


def my_place(size):
    return lax.rem(lax.axis_index("seq"), size)


def ones_where(keep):
    return jnp.where(keep, 1.0, 0.0).astype(BF16)


def running_sum(x, upper):
    rows = x.shape[0]
    parts = jnp.concatenate(three_parts(x), axis=0).astype(BF16)
    sums = dot(parts, upper)
    return sums[:rows] + sums[rows : 2 * rows] + sums[2 * rows :]


def diagonal(blocks):
    if len(blocks) == 1:
        return blocks[0]
    zero = jnp.zeros_like(blocks[0])
    rows = [[block if i == j else zero for j in range(len(blocks))] for i, block in enumerate(blocks)]
    return jnp.concatenate([jnp.concatenate(row, axis=1) for row in rows], axis=0)


def block_mask(table):
    length = table.shape[1]
    row = table[ROWS - 1 :, :]
    column = table.T[:, ROWS - 1 :]
    down = lax.broadcasted_iota(jnp.int32, (length, length), 0)
    across = lax.broadcasted_iota(jnp.int32, (length, length), 1)
    return jnp.where((across >= down) & (row == column), 0.0, MASKED)


class Plan:
    def __init__(self, heads, dim, length, size):
        self.heads, self.dim, self.length, self.size = heads, dim, length, size
        self.hpo = -(-heads // size)
        self.span = self.hpo * dim

    def lanes(self, slot):
        start = partner(my_place(self.size), slot, self.size) * self.span
        return pl.ds(pl.multiple_of(start, self.span), self.span)

    def head(self, i):
        return slice(i * self.dim, (i + 1) * self.dim)

    def tiles(self):
        for j in range(self.length // HALF):
            start = HALF * (j * (j + 1) // 2)
            yield slice(j * HALF, (j + 1) * HALF), slice(0, (j + 1) * HALF), slice(start, start + (j + 1) * HALF)

    def pairs(self):
        step = 2 if self.hpo % 2 == 0 else 1
        return [list(range(i, i + step)) for i in range(0, self.hpo, step)]

    def columns(self, pair):
        return slice(pair[0] * self.dim, (pair[-1] + 1) * self.dim)

    def guard(self, slot):
        return pl.when(partner(my_place(self.size), slot, self.size) * self.hpo < self.heads)


def order(size):
    return list(range(1, size)) + [0]


def arrival(size):
    return list(range(size))


def update_slot(plan, table, k_ref, v_ref, turned_ref, sent_ref):
    hpo, dim = plan.hpo, plan.dim
    line = lax.broadcasted_iota(jnp.int32, (ROWS, dim), 0)
    tile = jnp.zeros((ROWS, dim), F32)
    for i in range(hpo):
        lanes = plan.head(i)
        turned = k_ref[:, lanes].T
        turned_ref[lanes, :] = turned
        decayed = (turned.astype(F32) * table[2 * hpo + i : 2 * hpo + i + 1]).astype(BF16)
        sent_ref[lanes, :] = dot(decayed, v_ref[:, lanes]).astype(BF16)
        carry = jnp.broadcast_to(table[hpo + i : hpo + i + 1, plan.length - 1 :], (ROWS, dim))
        for j, part in enumerate(three_parts(carry)):
            tile = jnp.where(line == 3 * i + j, part, tile)
    sent_ref[hpo * dim :, :] = tile.astype(BF16)


def update_kernel(plan, logs_hbm, starts_hbm, k_hbm, v_hbm, *refs):
    size, hpo, heads, length = plan.size, plan.hpo, plan.heads, plan.length
    sent_refs, k_refs, v_refs, turned_refs = (refs[i * (size - 1) : (i + 1) * (size - 1)] for i in range(4))
    table_ref, logs_ref, starts_ref, natural_ref, small_sems, sems = refs[4 * (size - 1) :]
    copies = [
        pltpu.make_async_copy(logs_hbm, logs_ref, small_sems.at[0]),
        pltpu.make_async_copy(starts_hbm, starts_ref, small_sems.at[1]),
    ]
    for copy in copies:
        copy.start()

    def loads(slot):
        lanes = plan.lanes(slot)
        return (
            pltpu.make_async_copy(k_hbm.at[:, lanes], k_refs[slot - 1], sems.at[0, slot]),
            pltpu.make_async_copy(v_hbm.at[:, lanes], v_refs[slot - 1], sems.at[1, slot]),
        )

    for slot in range(1, size):

        @plan.guard(slot)
        def _():
            for copy in loads(slot):
                copy.start()

    down = lax.broadcasted_iota(jnp.int32, (length, length), 0)
    across = lax.broadcasted_iota(jnp.int32, (length, length), 1)
    upper = ones_where(down <= across)
    for copy in copies:
        copy.wait()
    flags = jnp.broadcast_to(starts_ref[...].astype(F32), (8, length))
    sums = running_sum(jnp.concatenate([logs_ref[...], flags], axis=0), upper)
    logs, count = sums[:heads] * LOG2E, sums[heads : heads + 1]
    last = slice(length - 1, length)
    enter = jnp.where(count == 0.0, jnp.exp2(logs), 0.0)
    leave = jnp.where(count == count[:, last], jnp.exp2(logs[:, last] - logs), 0.0)
    fill = jnp.broadcast_to(count, (ROWS - 3 * hpo, length))
    for owner in range(heads // hpo):
        rows = slice(owner * hpo, (owner + 1) * hpo)
        natural_ref[owner] = jnp.concatenate([logs[rows], enter[rows], leave[rows], fill], axis=0)
    table_ref[0] = natural_ref[jnp.minimum(my_place(size), heads // hpo - 1)]

    for slot in range(1, size):

        @plan.guard(slot)
        def _():
            table = natural_ref[partner(my_place(size), slot, size)]
            table_ref[slot] = table
            for copy in loads(slot):
                copy.wait()
            n = slot - 1
            update_slot(plan, table, k_refs[n], v_refs[n], turned_refs[n], sent_refs[n])


def scan_kernel(plan, forward, *refs):
    size, hpo, dim = plan.size, plan.hpo, plan.dim
    in_refs, refs = refs[:size], refs[size:]
    if forward:
        local_ref, total_ref, factor_ref, carry_ref, ordered_ref = refs[-5:]
    else:
        carry_ref = refs[0]
        local_ref, total_ref, factor_ref, ordered_ref = refs[-4:]
    me = my_place(size)
    for slot, in_ref in enumerate(in_refs):
        ordered_ref[inverse(me, slot, size)] = in_ref[...]
    if forward:
        for b in range(size):
            tile = ordered_ref[b, hpo * dim :, :].astype(F32)
            for i in range(hpo):
                carry_ref[b, i : i + 1, :] = tile[3 * i : 3 * i + 1] + tile[3 * i + 1 : 3 * i + 2] + tile[3 * i + 2 : 3 * i + 3]
    for i in range(hpo):
        rows = plan.head(i)
        state = jnp.zeros((dim, dim), F32)
        factor = jnp.ones((1, dim), F32)
        for b in range(size) if forward else reversed(range(size)):
            carry = carry_ref[b, i : i + 1, :]
            local_ref[b, rows, :] = state
            factor_ref[b, i : i + 1, :] = factor
            state = carry * state + ordered_ref[b, rows, :].astype(F32)
            factor = factor * carry
        total_ref[rows, :] = state.astype(BF16)


def return_kernel(plan, forward, local_ref, factor_ref, outer_ref, *refs):
    out_refs = refs[-plan.size :]
    me = my_place(plan.size)
    upper = lax.axis_index("seq") >= plan.size
    takes = upper if forward else jnp.logical_not(upper)
    for i in range(plan.hpo):
        rows = plan.head(i)
        outer = jnp.where(takes, outer_ref[rows, :].astype(F32), 0.0)
        for slot, out_ref in enumerate(out_refs):
            b = inverse(me, slot, plan.size)
            out_ref[rows, :] = (local_ref[b, rows, :] + factor_ref[b, i : i + 1, :] * outer).astype(BF16)


def intra_kernel(plan, slot, first_part, table_ref, *refs):
    size, hpo, length = plan.size, plan.hpo, plan.length
    copies = []
    if first_part:
        q_hbm, cot_hbm, k_hbm, v_hbm, k_ref, v_ref, turned_ref, sent_ref = refs[:8]
        q_refs, cot_refs = refs[8 : 8 + size], refs[8 + size : 8 + 2 * size]
        mask_ref, out_ref, decayed_ref, probs_ref, weight_ref, sems = refs[8 + 2 * size :]
        q_ref = q_refs[slot]
        first = [(slot, k_hbm, k_ref), (slot, v_hbm, v_ref), (slot, q_hbm, q_ref)]
        rest = [(other, q_hbm, q_refs[other]) for other in range(size) if other != slot]
        rest += [(other, cot_hbm, cot_refs[other]) for other in range(size)]
        copies = [
            (other, pltpu.make_async_copy(source.at[:, plan.lanes(other)], target, sems.at[n]))
            for n, (other, source, target) in enumerate(first + rest)
        ]
        start_all(plan, copies)
        mask_ref[...] = block_mask(table_ref[0])
        wait_all(plan, copies[:3])
    else:
        k_ref, v_ref, q_ref, mask_ref, out_ref, decayed_ref, probs_ref, weight_ref = refs

    @plan.guard(slot)
    def _():
        table = table_ref[slot]
        columns = table.T
        if first_part:
            update_slot(plan, table, k_ref, v_ref, turned_ref, sent_ref)
        for i in range(hpo):
            lanes = plan.head(i)
            turned = q_ref[:, lanes].T
            decayed_ref[lanes, :] = (turned.astype(F32) * table[hpo + i : hpo + i + 1]).astype(BF16)
            for later, seen, kept in plan.tiles():
                gap = table[i : i + 1, later] - columns[seen, i : i + 1]
                weight = jnp.exp2(gap + mask_ref[seen, later])
                probs = (dot(k_ref[seen, lanes], turned[:, later]) * weight).astype(BF16)
                weight_ref[i, kept, :] = weight.astype(BF16)
                probs_ref[i, kept, :] = probs
                out_ref[later, lanes] = dot(probs, v_ref[seen, lanes], ((0,), (0,)))

    wait_all(plan, copies[3:])


def token_rows(total):
    rows = [jnp.sum(total[i : i + 128].T, axis=0, keepdims=True) for i in range(0, total.shape[0], 128)]
    return jnp.concatenate(rows, axis=0)


def sums_kernel(total_ref, sums_ref):
    sums_ref[...] = jnp.concatenate([token_rows(total_ref[0]), token_rows(total_ref[1])], axis=0)


def output_kernel(plan, slot, first_part, table_ref, q_ref, cot_ref, intra_ref, state_ref, *refs):
    hpo = plan.hpo
    if not first_part:
        old_ref, refs = refs[0], refs[1:]
    out_ref, total_ref = refs[:2]
    if first_part:
        total_ref[...] = jnp.zeros_like(total_ref)
    else:
        total_ref[...] = old_ref[...]

    @plan.guard(slot)
    def _():
        columns = table_ref[slot].T
        square, cross = total_ref[0], total_ref[1]
        for pair in plan.pairs():
            states = diagonal([state_ref[plan.head(i), :] for i in pair])
            both = dot(q_ref[:, plan.columns(pair)], states)
            for j, i in enumerate(pair):
                lanes = plan.head(i)
                out = intra_ref[:, lanes] + columns[:, hpo + i : hpo + i + 1] * both[:, plan.head(j)]
                out_ref[:, lanes] = out
                square = square + out * out
                cross = cross + cot_ref[:, lanes].astype(F32) * out
        total_ref[0] = square
        total_ref[1] = cross


def factors(sums_refs, factor_ref):
    total = sums_refs[0][...]
    for ref in sums_refs[1:]:
        total = total + ref[...]
    lines = total.shape[0] // 2
    full = HEAD_TOTAL * HEAD_DIM
    scale = lax.rsqrt(total[:lines] / full + EPS)
    slope = scale * scale * scale * total[lines:] / full
    turned = jnp.concatenate([scale, slope], axis=0).T
    for j in range(2):
        for i in range(lines):
            column = turned[:, j * lines + i : j * lines + i + 1]
            factor_ref[j, i * 128 : (i + 1) * 128, :] = jnp.broadcast_to(column, (128, factor_ref.shape[2]))


def gout_kernel(plan, slot, count, *refs):
    if count:
        factor_ref = refs[count + 3]
        factors(refs[:count], factor_ref)
        out_ref, cot_ref, decayed_ref, _, gout_ref, sent_ref = refs[count:]
    else:
        factor_ref, out_ref, cot_ref, decayed_ref, gout_ref, sent_ref = refs

    @plan.guard(slot)
    def _():
        for i in range(plan.hpo):
            lanes = plan.head(i)
            gout = factor_ref[0] * cot_ref[:, lanes].astype(F32) - factor_ref[1] * out_ref[:, lanes]
            gout = gout.astype(BF16)
            gout_ref[:, lanes] = gout
            sent_ref[lanes, :] = dot(decayed_ref[lanes, :], gout).astype(BF16)


def attn_kernel(plan, factor_ref, *refs):
    size = plan.size
    for slot, (out_ref, attn_ref) in enumerate(zip(refs[:size], refs[size:])):

        @plan.guard(slot)
        def _():
            for i in range(plan.hpo):
                lanes = plan.head(i)
                attn_ref[:, lanes] = (factor_ref[0] * out_ref[:, lanes]).astype(BF16)


def stores(plan, slots, in_refs, hbms, sems):
    return [
        (slot, pltpu.make_async_copy(ref, hbm.at[:, plan.lanes(slot)], sems.at[n]))
        for n, (slot, ref, hbm) in enumerate(zip(slots, in_refs, hbms))
    ]


def start_all(plan, copies):
    for slot, copy in copies:
        plan.guard(slot)(copy.start)


def wait_all(plan, copies):
    for slot, copy in copies:
        plan.guard(slot)(copy.wait)


def gradient_kernel(plan, slot, finished, fresh, *refs):
    table_ref, k_ref, v_ref, q_ref, gout_ref, turned_ref, probs_ref, weight_ref, state_ref = refs[:9]
    refs = refs[9:]
    done_refs, refs = refs[: len(finished)], refs[len(finished) :]
    copies = []
    if finished:
        if not fresh:
            refs = refs[1:]
        copies = stores(plan, finished, done_refs, [refs[0]] * len(finished), refs[-1])
        refs = refs[1:-1]
    start_all(plan, copies)
    gq_ref, gk_ref, gv_ref = refs
    hpo, length = plan.hpo, plan.length

    @plan.guard(slot)
    def _():
        table = table_ref[slot]
        for i in range(hpo):
            lanes = plan.head(i)
            gout_turned = gout_ref[:, lanes].T
            carried = table[hpo + i : hpo + i + 1] * dot(state_ref[lanes, :], gout_turned)
            tiles = list(plan.tiles())
            grads = [None] * len(tiles)
            for j, (later, seen, kept) in reversed(list(enumerate(tiles))):
                product = dot(v_ref[seen, lanes], gout_turned[:, later])
                grads[j] = (product * weight_ref[i, kept, :].astype(F32)).astype(BF16)
            probs = [probs_ref[i, kept, :] for _, _, kept in tiles]
            for target, lefts, right_ref in ((gv_ref, probs, gout_ref), (gk_ref, grads, q_ref)):
                parts = [dot(left, right_ref[later, lanes]) for left, (later, _, _) in zip(lefts, tiles)]
                for j, (rows, _, _) in enumerate(tiles):
                    target[rows, lanes] = functools.reduce(jnp.add, [part[rows] for part in reversed(parts[j:])])
            for grad, (later, seen, _) in zip(grads, tiles):
                total = carried[:, later] + dot(turned_ref[lanes, seen], grad)
                gq_ref[later, lanes] = total.astype(BF16).T

    wait_all(plan, copies)


def final_kernel(plan, slot, finished, fresh, last_part, *refs):
    table_ref, k_ref, v_ref, gkp_ref, gvp_ref, back_ref = refs[:6]
    refs = refs[6:]
    done_refs, refs = refs[: len(finished)], refs[len(finished) :]
    if not all(fresh):
        refs = refs[fresh.count(False) :]
    gq_hbm, gk_hbm, gv_hbm, gk_ref, gv_ref, sems = refs
    hbm_of = {"gq": gq_hbm, "gk": gk_hbm, "gv": gv_hbm}
    copies = stores(plan, [s for _, s in finished], done_refs, [hbm_of[name] for name, _ in finished], sems)
    start_all(plan, copies)

    tails = []
    if last_part:
        for n, pair in enumerate(plan.pairs()):
            for m, (ref, target) in enumerate(((gk_ref, gk_hbm), (gv_ref, gv_hbm))):
                start = partner(my_place(plan.size), slot, plan.size) * plan.span
                width = len(pair) * plan.dim
                lanes = pl.ds(pl.multiple_of(start + n * width, width), width)
                sem = sems.at[len(finished) + 2 * n + m]
                tails.append((slot, pltpu.make_async_copy(ref.at[:, plan.columns(pair)], target.at[:, lanes], sem)))

    @plan.guard(slot)
    def _():
        columns = table_ref[slot].T
        for n, pair in enumerate(plan.pairs()):
            back = diagonal([back_ref[plan.head(i), :] for i in pair])
            both = plan.columns(pair)
            from_values = dot_nt(v_ref[:, both], back)
            from_keys = dot(k_ref[:, both], back)
            for j, i in enumerate(pair):
                lanes, part = plan.head(i), plan.head(j)
                leave = columns[:, 2 * plan.hpo + i : 2 * plan.hpo + i + 1]
                gk_ref[:, lanes] = (gkp_ref[:, lanes] + leave * from_values[:, part]).astype(BF16)
                gv_ref[:, lanes] = (gvp_ref[:, lanes] + leave * from_keys[:, part]).astype(BF16)
            for _, copy in tails[2 * n : 2 * n + 2]:
                copy.start()

    wait_all(plan, copies + tails)


def exchange(arrays, size, halves, target):
    def pairs(slot):
        return [(base + i, base + target(i, slot, size)) for base in range(0, halves * size, size) for i in range(size)]

    return [arrays[0]] + [lax.ppermute(arrays[slot], "seq", pairs(slot)) for slot in range(1, size)]


def per_device(queries, keys, values, cotangent, log_decay, starts):
    length, width = queries.shape
    heads = log_decay.shape[0]
    dim = width // heads
    blocks = lax.axis_size("seq")
    shares = lax.axis_size("head")
    halves = 2 if blocks % 2 == 0 else 1
    size = blocks // halves
    plan = Plan(heads, dim, length, size)
    hpo, span = plan.hpo, plan.span
    params = pltpu.CompilerParams(vmem_limit_bytes=12 << 20)

    inside = pl.BlockSpec(memory_space=pltpu.VMEM)
    unused = pl.BlockSpec(memory_space=pl.ANY)
    hbm = pl.BlockSpec(memory_space=pltpu.HBM)
    dma = pltpu.SemaphoreType.DMA
    whole = pltpu.HBM((length, width), BF16)

    def outside(array):
        return pltpu.with_memory_space_constraint(array, pltpu.HBM)

    def held(dtype, columns=span):
        return pltpu.VMEM((length, columns), dtype)

    def cost(products, exps=0):
        return pl.CostEstimate(flops=2 * hpo * products, bytes_accessed=length * span, transcendentals=hpo * exps)

    def call(kernel, name, operands, results, work, extra=(), scratch=(), aliases=None):
        far = [isinstance(a, tuple) for a in operands]
        return pl.pallas_call(
            kernel,
            in_specs=[hbm if f else inside for f in far] + [unused] * len(extra),
            out_specs=[hbm if r is whole else inside for r in results],
            out_shape=list(results),
            scratch_shapes=list(scratch),
            input_output_aliases=aliases or {},
            compiler_params=params,
            cost_estimate=work,
            name=name,
        )(*[a[0] if f else a for a, f in zip(operands, far)], *extra)

    def scan(arrays, carries, after, later):
        forward = carries is None
        factor = pltpu.VMEM((size, 8, dim), F32)
        local, total, factor, *rest = call(
            functools.partial(scan_kernel, plan, forward),
            "scan",
            [*arrays] + ([] if forward else [carries]),
            [pltpu.VMEM((size, span, dim), F32), pltpu.VMEM((span, dim), BF16), factor] + ([factor] if forward else []),
            None,
            after,
            [pltpu.VMEM((size, *arrays[0].shape), BF16)],
        )
        if halves == 2:
            pairs = [(i, (i + size) % (2 * size)) for i in range(2 * size)]
            outer = lax.ppermute(total, "seq", pairs)
        else:
            outer = jnp.zeros_like(total)
        back = call(
            functools.partial(return_kernel, plan, forward),
            "return",
            [local, factor, outer],
            [pltpu.VMEM((span, dim), BF16)] * size,
            None,
            later,
        )
        return exchange(back, size, halves, inverse), (rest[0] if forward else None)

    big, small = length * length * dim, length * dim * dim
    queries, keys, values, cotangent = (outside(a) for a in (queries, keys, values, cotangent))
    others = size - 1
    results = call(
        functools.partial(update_kernel, plan),
        "update",
        [(outside(log_decay),), (outside(starts.reshape(1, length)),), (keys,), (values,)],
        [pltpu.VMEM((span + ROWS, dim), BF16)] * others
        + [held(BF16)] * (2 * others)
        + [pltpu.VMEM((span, length), BF16)] * others
        + [pltpu.VMEM((size, ROWS, length), F32)],
        cost(size * small),
        scratch=[
            pltpu.VMEM((heads, length), F32),
            pltpu.VMEM((1, length), jnp.int32),
            pltpu.VMEM((heads // hpo, ROWS, length), F32),
            dma((2,)),
            dma((2, size)),
        ],
    )
    sent, k, v, turned = ([None, *results[i * others : (i + 1) * others]] for i in range(4))
    table = results[-1]
    received = exchange(sent, size, halves, partner)
    own = [held(BF16)] * 2 + [pltpu.VMEM((span, length), BF16), pltpu.VMEM((span + ROWS, dim), BF16)]

    kept = pltpu.VMEM((hpo, length * (length + HALF) // 2 // HALF, HALF), BF16)
    intra, decayed, probs, weights = [], [], [], []
    for slot in range(size):
        first = slot == 0
        results = call(
            functools.partial(intra_kernel, plan, slot, first),
            "intra",
            [table] + ([(a,) for a in (queries, cotangent, keys, values)] if first else [k[slot], v[slot], q[slot], mask]),
            (own + [held(BF16)] * (2 * size) + [pltpu.VMEM((length, length), F32)] if first else [])
            + [held(F32), pltpu.VMEM((span, length), BF16), kept, kept],
            cost(2 * big, length * length),
            scratch=[dma((2 + 2 * size,))] if first else [],
        )
        if first:
            k[0], v[0], turned[0], sent[0], *results = results
            q, cot, mask = results[:size], results[size : 2 * size], results[2 * size]
        for kind, result in zip((intra, decayed, probs, weights), results[-4:]):
            kind.append(result)

    middle = -(-size // 2)
    received[0] = sent[0]
    received, carries = scan(received, None, intra[:middle], intra[middle:])

    outputs = [None] * size
    total = None
    for slot in arrival(size):
        first = slot == 0
        outputs[slot], total = call(
            functools.partial(output_kernel, plan, slot, first),
            "output",
            [table, q[slot], cot[slot], intra[slot], received[slot]] + ([] if first else [total]),
            [held(F32), pltpu.VMEM((2, length, dim), F32)],
            cost(small),
        )
    (sums,) = call(sums_kernel, "sums", [total], [pltpu.VMEM((2 * length // 128, 128), F32)], cost(length))
    states = received

    everyone = [sums] + [
        lax.ppermute(sums, "head", [(i, partner(i, k, shares)) for i in range(shares)]) for k in [*range(2, shares), 1]
    ]

    gout, sent = [None] * size, [None] * size
    factor = None
    for slot in order(size):
        first = factor is None
        *rest, gout[slot], sent[slot] = call(
            functools.partial(gout_kernel, plan, slot, shares if first else 0),
            "gout",
            (everyone if first else [factor]) + [outputs[slot], cot[slot], decayed[slot]],
            ([pltpu.VMEM((2, length, dim), F32)] if first else []) + [held(BF16), pltpu.VMEM((span, dim), BF16)],
            cost(small),
        )
        factor = rest[0] if first else factor
    received = exchange(sent, size, halves, partner)
    attn = call(
        functools.partial(attn_kernel, plan),
        "attn",
        [factor, *outputs],
        [held(BF16)] * size,
        cost(small),
    )

    gq, gk_part, gv_part = [], [], []
    attn_whole = gq_whole = None
    for slot in range(size):
        fresh = slot < 2
        finished = list(range(size)) if slot == 0 else [slot - 1]
        done = list(attn) if slot == 0 else [gq[slot - 1]]
        operands = [table, k[slot], v[slot], q[slot], gout[slot], turned[slot], probs[slot], weights[slot], states[slot]]
        operands += done
        results = call(
            functools.partial(gradient_kernel, plan, slot, finished, fresh),
            "gradient",
            operands + ([] if fresh else [(gq_whole,)]),
            [whole, held(BF16), held(F32), held(F32)],
            cost(4 * big),
            scratch=[dma((len(finished),))],
            aliases={} if fresh else {len(operands): 0},
        )
        if slot == 0:
            attn_whole = results[0]
        else:
            gq_whole = results[0]
        for kind, result in zip((gq, gk_part, gv_part), results[1:]):
            kind.append(result)

    received, _ = scan(received, carries, gk_part[:1], gk_part[1:-1])

    gk_whole = gv_whole = None
    gk = gv = None
    slots = arrival(size)
    for n, slot in enumerate(slots):
        first, last = n == 0, n == size - 1
        finished = [("gq", size - 1)] if first else [("gk", slots[n - 1]), ("gv", slots[n - 1])]
        done = [gq[-1]] if first else [gk, gv]
        operands = [table, k[slot], v[slot], gk_part[slot], gv_part[slot], received[slot]] + done
        held_back = [gq_whole, gk_whole, gv_whole]
        fresh = [a is None for a in held_back]
        aliases = {}
        chained = []
        for m, array in enumerate(held_back):
            if array is not None:
                aliases[len(operands) + len(chained)] = m
                chained.append((array,))
        gq_whole, gk_whole, gv_whole, gk, gv = call(
            functools.partial(final_kernel, plan, slot, finished, fresh, last),
            "final",
            operands + chained,
            [whole] * 3 + [held(BF16)] * 2,
            cost(2 * small),
            scratch=[dma((len(finished) + 2 * len(plan.pairs()),))],
            aliases=aliases,
        )
    return (attn_whole, gq_whole, gk_whole, gv_whole)


def solution(mesh):
    wide = P("seq", "head")
    return jax.shard_map(
        per_device,
        mesh=mesh,
        in_specs=(wide, wide, wide, wide, P("head", "seq"), P("seq")),
        out_specs=(wide, wide, wide, wide),
        check_vma=False,
    )
```

```python
import functools

import jax
import jax.numpy as jnp
from jax import lax
from jax.experimental import pallas as pl
from jax.experimental.pallas import tpu as pltpu
from jax.sharding import PartitionSpec as P

HEAD_TOTAL = 64
HEAD_DIM = 128
EPS = 1e-05
LOG2E = 1.4426950408889634
MASKED = -1e30
ROWS = 16
HALF = 256
F32 = jnp.float32
BF16 = jnp.bfloat16


def dot(a, b, dims=((1,), (0,))):
    return lax.dot_general(a, b, (dims, ((), ())), preferred_element_type=F32)


def dot_nt(a, b):
    return dot(a, b, ((1,), (1,)))


def three_parts(x):
    high = x.astype(BF16).astype(F32)
    rest = x - high
    middle = rest.astype(BF16).astype(F32)
    return high, middle, rest - middle


def lanes_of(index, size):
    return pl.ds(index * size if isinstance(index, int) else pl.multiple_of(index * size, size), size)


def partner(place, slot, size):
    if size & (size - 1):
        return (place + slot) % size
    return place ^ (3 - slot if slot in (1, 2) and size > 2 else slot)


def inverse(place, slot, size):
    return partner(place, slot, size) if size & (size - 1) == 0 else (place + size - slot) % size


def mirrored(place, half, size):
    return place ^ (2 * half) if size == 4 else place


def my_place(size):
    return lax.rem(lax.axis_index("seq"), size)


def ones_where(keep):
    return jnp.where(keep, 1.0, 0.0).astype(BF16)


def running_sum(x, upper):
    rows = x.shape[0]
    parts = jnp.concatenate(three_parts(x), axis=0).astype(BF16)
    sums = dot(parts, upper)
    return sums[:rows] + sums[rows : 2 * rows] + sums[2 * rows :]


def diagonal(blocks):
    if len(blocks) == 1:
        return blocks[0]
    zero = jnp.zeros_like(blocks[0])
    rows = [[block if i == j else zero for j in range(len(blocks))] for i, block in enumerate(blocks)]
    return jnp.concatenate([jnp.concatenate(row, axis=1) for row in rows], axis=0)


def block_mask(table):
    length = table.shape[1]
    row = table[ROWS - 1 :, :]
    column = table.T[:, ROWS - 1 :]
    down = lax.broadcasted_iota(jnp.int32, (length, length), 0)
    across = lax.broadcasted_iota(jnp.int32, (length, length), 1)
    return jnp.where((across >= down) & (row == column), 0.0, MASKED)


class Plan:
    def __init__(self, heads, dim, length, size):
        self.heads, self.dim, self.length, self.size = heads, dim, length, size
        self.hpo = -(-heads // size)
        self.span = self.hpo * dim

    def owner(self, slot):
        return mirrored(partner(my_place(self.size), slot, self.size), lax.axis_index("seq") // self.size, self.size)

    def lanes(self, slot):
        start = self.owner(slot) * self.span
        return pl.ds(pl.multiple_of(start, self.span), self.span)

    def head(self, i):
        return slice(i * self.dim, (i + 1) * self.dim)

    def tiles(self):
        for j in range(self.length // HALF):
            start = HALF * (j * (j + 1) // 2)
            yield slice(j * HALF, (j + 1) * HALF), slice(0, (j + 1) * HALF), slice(start, start + (j + 1) * HALF)

    def pairs(self):
        step = 2 if self.hpo % 2 == 0 else 1
        return [list(range(i, i + step)) for i in range(0, self.hpo, step)]

    def columns(self, pair):
        return slice(pair[0] * self.dim, (pair[-1] + 1) * self.dim)

    def guard(self, slot):
        return pl.when(self.owner(slot) * self.hpo < self.heads)


def order(size):
    return list(range(1, size)) + [0]


def arrival(size):
    return list(range(size))


def update_slot(plan, table, k_ref, v_ref, turned_ref, sent_ref):
    hpo, dim = plan.hpo, plan.dim
    line = lax.broadcasted_iota(jnp.int32, (ROWS, dim), 0)
    tile = jnp.zeros((ROWS, dim), F32)
    for i in range(hpo):
        lanes = plan.head(i)
        turned = k_ref[:, lanes].T
        turned_ref[lanes, :] = turned
        decayed = (turned.astype(F32) * table[2 * hpo + i : 2 * hpo + i + 1]).astype(BF16)
        sent_ref[lanes, :] = dot(decayed, v_ref[:, lanes]).astype(BF16)
        carry = jnp.broadcast_to(table[hpo + i : hpo + i + 1, plan.length - 1 :], (ROWS, dim))
        for j, part in enumerate(three_parts(carry)):
            tile = jnp.where(line == 3 * i + j, part, tile)
    sent_ref[hpo * dim :, :] = tile.astype(BF16)


def update_kernel(plan, logs_hbm, starts_hbm, k_hbm, v_hbm, *refs):
    size, hpo, heads, length = plan.size, plan.hpo, plan.heads, plan.length
    sent_refs, k_refs, v_refs, turned_refs = (refs[i * (size - 1) : (i + 1) * (size - 1)] for i in range(4))
    table_ref, logs_ref, starts_ref, natural_ref, small_sems, sems = refs[4 * (size - 1) :]
    copies = [
        pltpu.make_async_copy(logs_hbm, logs_ref, small_sems.at[0]),
        pltpu.make_async_copy(starts_hbm, starts_ref, small_sems.at[1]),
    ]
    for copy in copies:
        copy.start()

    def loads(slot):
        lanes = plan.lanes(slot)
        return (
            pltpu.make_async_copy(k_hbm.at[:, lanes], k_refs[slot - 1], sems.at[0, slot]),
            pltpu.make_async_copy(v_hbm.at[:, lanes], v_refs[slot - 1], sems.at[1, slot]),
        )

    for slot in range(1, size):

        @plan.guard(slot)
        def _():
            for copy in loads(slot):
                copy.start()

    down = lax.broadcasted_iota(jnp.int32, (length, length), 0)
    across = lax.broadcasted_iota(jnp.int32, (length, length), 1)
    upper = ones_where(down <= across)
    for copy in copies:
        copy.wait()
    flags = jnp.broadcast_to(starts_ref[...].astype(F32), (8, length))
    sums = running_sum(jnp.concatenate([logs_ref[...], flags], axis=0), upper)
    logs, count = sums[:heads] * LOG2E, sums[heads : heads + 1]
    last = slice(length - 1, length)
    enter = jnp.where(count == 0.0, jnp.exp2(logs), 0.0)
    leave = jnp.where(count == count[:, last], jnp.exp2(logs[:, last] - logs), 0.0)
    fill = jnp.broadcast_to(count, (ROWS - 3 * hpo, length))
    for owner in range(heads // hpo):
        rows = slice(owner * hpo, (owner + 1) * hpo)
        natural_ref[owner] = jnp.concatenate([logs[rows], enter[rows], leave[rows], fill], axis=0)
    table_ref[0] = natural_ref[jnp.minimum(plan.owner(0), heads // hpo - 1)]

    for slot in range(1, size):

        @plan.guard(slot)
        def _():
            table = natural_ref[plan.owner(slot)]
            table_ref[slot] = table
            for copy in loads(slot):
                copy.wait()
            n = slot - 1
            update_slot(plan, table, k_refs[n], v_refs[n], turned_refs[n], sent_refs[n])


def scan_kernel(plan, forward, *refs):
    size, hpo, dim = plan.size, plan.hpo, plan.dim
    in_refs, refs = refs[:size], refs[size:]
    if forward:
        local_ref, total_ref, factor_ref, carry_ref, ordered_ref = refs[-5:]
    else:
        carry_ref = refs[0]
        local_ref, total_ref, factor_ref, ordered_ref = refs[-4:]
    me = my_place(size)
    for slot, in_ref in enumerate(in_refs):
        ordered_ref[inverse(me, slot, size)] = in_ref[...]
    if forward:
        for b in range(size):
            tile = ordered_ref[b, hpo * dim :, :].astype(F32)
            for i in range(hpo):
                carry_ref[b, i : i + 1, :] = tile[3 * i : 3 * i + 1] + tile[3 * i + 1 : 3 * i + 2] + tile[3 * i + 2 : 3 * i + 3]
    for i in range(hpo):
        rows = plan.head(i)
        state = jnp.zeros((dim, dim), F32)
        factor = jnp.ones((1, dim), F32)
        for b in range(size) if forward else reversed(range(size)):
            carry = carry_ref[b, i : i + 1, :]
            local_ref[b, rows, :] = state
            factor_ref[b, i : i + 1, :] = factor
            state = carry * state + ordered_ref[b, rows, :].astype(F32)
            factor = factor * carry
        total_ref[rows, :] = state.astype(BF16)


def return_kernel(plan, forward, local_ref, factor_ref, outer_ref, *refs):
    out_refs = refs[-plan.size :]
    me = my_place(plan.size)
    upper = lax.axis_index("seq") >= plan.size
    takes = upper if forward else jnp.logical_not(upper)
    for i in range(plan.hpo):
        rows = plan.head(i)
        outer = jnp.where(takes, outer_ref[rows, :].astype(F32), 0.0)
        for slot, out_ref in enumerate(out_refs):
            b = inverse(me, slot, plan.size)
            out_ref[rows, :] = (local_ref[b, rows, :] + factor_ref[b, i : i + 1, :] * outer).astype(BF16)


def intra_kernel(plan, slot, first_part, table_ref, *refs):
    size, hpo, length = plan.size, plan.hpo, plan.length
    copies = []
    if first_part:
        q_hbm, cot_hbm, k_hbm, v_hbm, k_ref, v_ref, turned_ref, sent_ref = refs[:8]
        q_refs, cot_refs = refs[8 : 8 + size], refs[8 + size : 8 + 2 * size]
        mask_ref, out_ref, decayed_ref, probs_ref, weight_ref, sems = refs[8 + 2 * size :]
        q_ref = q_refs[slot]
        first = [(slot, k_hbm, k_ref), (slot, v_hbm, v_ref), (slot, q_hbm, q_ref)]
        rest = [(other, q_hbm, q_refs[other]) for other in range(size) if other != slot]
        rest += [(other, cot_hbm, cot_refs[other]) for other in range(size)]
        copies = [
            (other, pltpu.make_async_copy(source.at[:, plan.lanes(other)], target, sems.at[n]))
            for n, (other, source, target) in enumerate(first + rest)
        ]
        start_all(plan, copies)
        mask_ref[...] = block_mask(table_ref[0])
        wait_all(plan, copies[:3])
    else:
        k_ref, v_ref, q_ref, mask_ref, out_ref, decayed_ref, probs_ref, weight_ref = refs

    @plan.guard(slot)
    def _():
        table = table_ref[slot]
        columns = table.T
        if first_part:
            update_slot(plan, table, k_ref, v_ref, turned_ref, sent_ref)
        for i in range(hpo):
            lanes = plan.head(i)
            turned = q_ref[:, lanes].T
            decayed_ref[lanes, :] = (turned.astype(F32) * table[hpo + i : hpo + i + 1]).astype(BF16)
            for later, seen, kept in plan.tiles():
                gap = table[i : i + 1, later] - columns[seen, i : i + 1]
                weight = jnp.exp2(gap + mask_ref[seen, later])
                probs = (dot(k_ref[seen, lanes], turned[:, later]) * weight).astype(BF16)
                weight_ref[i, kept, :] = weight.astype(BF16)
                probs_ref[i, kept, :] = probs
                out_ref[later, lanes] = dot(probs, v_ref[seen, lanes], ((0,), (0,)))

    wait_all(plan, copies[3:])


def token_rows(total):
    rows = [jnp.sum(total[i : i + 128].T, axis=0, keepdims=True) for i in range(0, total.shape[0], 128)]
    return jnp.concatenate(rows, axis=0)


def sums_kernel(total_ref, sums_ref):
    sums_ref[...] = jnp.concatenate([token_rows(total_ref[0]), token_rows(total_ref[1])], axis=0)


def output_kernel(plan, slot, first_part, table_ref, q_ref, cot_ref, intra_ref, state_ref, *refs):
    hpo = plan.hpo
    if not first_part:
        old_ref, refs = refs[0], refs[1:]
    out_ref, total_ref = refs[:2]
    if first_part:
        total_ref[...] = jnp.zeros_like(total_ref)
    else:
        total_ref[...] = old_ref[...]

    @plan.guard(slot)
    def _():
        columns = table_ref[slot].T
        square, cross = total_ref[0], total_ref[1]
        for pair in plan.pairs():
            states = diagonal([state_ref[plan.head(i), :] for i in pair])
            both = dot(q_ref[:, plan.columns(pair)], states)
            for j, i in enumerate(pair):
                lanes = plan.head(i)
                out = intra_ref[:, lanes] + columns[:, hpo + i : hpo + i + 1] * both[:, plan.head(j)]
                out_ref[:, lanes] = out
                square = square + out * out
                cross = cross + cot_ref[:, lanes].astype(F32) * out
        total_ref[0] = square
        total_ref[1] = cross


def factors(sums_refs, factor_ref):
    total = sums_refs[0][...]
    for ref in sums_refs[1:]:
        total = total + ref[...]
    lines = total.shape[0] // 2
    full = HEAD_TOTAL * HEAD_DIM
    scale = lax.rsqrt(total[:lines] / full + EPS)
    slope = scale * scale * scale * total[lines:] / full
    turned = jnp.concatenate([scale, slope], axis=0).T
    for j in range(2):
        for i in range(lines):
            column = turned[:, j * lines + i : j * lines + i + 1]
            factor_ref[j, i * 128 : (i + 1) * 128, :] = jnp.broadcast_to(column, (128, factor_ref.shape[2]))


def gout_kernel(plan, slot, count, *refs):
    if count:
        factor_ref = refs[count + 3]
        factors(refs[:count], factor_ref)
        out_ref, cot_ref, decayed_ref, _, gout_ref, sent_ref = refs[count:]
    else:
        factor_ref, out_ref, cot_ref, decayed_ref, gout_ref, sent_ref = refs

    @plan.guard(slot)
    def _():
        for i in range(plan.hpo):
            lanes = plan.head(i)
            gout = factor_ref[0] * cot_ref[:, lanes].astype(F32) - factor_ref[1] * out_ref[:, lanes]
            gout = gout.astype(BF16)
            gout_ref[:, lanes] = gout
            sent_ref[lanes, :] = dot(decayed_ref[lanes, :], gout).astype(BF16)


def attn_kernel(plan, factor_ref, *refs):
    size = plan.size
    for slot, (out_ref, attn_ref) in enumerate(zip(refs[:size], refs[size:])):

        @plan.guard(slot)
        def _():
            for i in range(plan.hpo):
                lanes = plan.head(i)
                attn_ref[:, lanes] = (factor_ref[0] * out_ref[:, lanes]).astype(BF16)


def stores(plan, slots, in_refs, hbms, sems):
    return [
        (slot, pltpu.make_async_copy(ref, hbm.at[:, plan.lanes(slot)], sems.at[n]))
        for n, (slot, ref, hbm) in enumerate(zip(slots, in_refs, hbms))
    ]


def start_all(plan, copies):
    for slot, copy in copies:
        plan.guard(slot)(copy.start)


def wait_all(plan, copies):
    for slot, copy in copies:
        plan.guard(slot)(copy.wait)


def gradient_kernel(plan, slot, finished, fresh, *refs):
    table_ref, k_ref, v_ref, q_ref, gout_ref, turned_ref, probs_ref, weight_ref, state_ref = refs[:9]
    refs = refs[9:]
    done_refs, refs = refs[: len(finished)], refs[len(finished) :]
    copies = []
    if finished:
        if not fresh:
            refs = refs[1:]
        copies = stores(plan, finished, done_refs, [refs[0]] * len(finished), refs[-1])
        refs = refs[1:-1]
    start_all(plan, copies)
    gq_ref, gk_ref, gv_ref = refs
    hpo, length = plan.hpo, plan.length

    @plan.guard(slot)
    def _():
        table = table_ref[slot]
        for i in range(hpo):
            lanes = plan.head(i)
            gout_turned = gout_ref[:, lanes].T
            carried = table[hpo + i : hpo + i + 1] * dot(state_ref[lanes, :], gout_turned)
            tiles = list(plan.tiles())
            grads = [None] * len(tiles)
            for j, (later, seen, kept) in reversed(list(enumerate(tiles))):
                product = dot(v_ref[seen, lanes], gout_turned[:, later])
                grads[j] = (product * weight_ref[i, kept, :].astype(F32)).astype(BF16)
            probs = [probs_ref[i, kept, :] for _, _, kept in tiles]
            for target, lefts, right_ref in ((gv_ref, probs, gout_ref), (gk_ref, grads, q_ref)):
                parts = [dot(left, right_ref[later, lanes]) for left, (later, _, _) in zip(lefts, tiles)]
                for j, (rows, _, _) in enumerate(tiles):
                    target[rows, lanes] = functools.reduce(jnp.add, [part[rows] for part in reversed(parts[j:])])
            for grad, (later, seen, _) in zip(grads, tiles):
                total = carried[:, later] + dot(turned_ref[lanes, seen], grad)
                gq_ref[later, lanes] = total.astype(BF16).T

    wait_all(plan, copies)


def final_kernel(plan, slot, finished, fresh, last_part, *refs):
    table_ref, k_ref, v_ref, gkp_ref, gvp_ref, back_ref = refs[:6]
    refs = refs[6:]
    done_refs, refs = refs[: len(finished)], refs[len(finished) :]
    if not all(fresh):
        refs = refs[fresh.count(False) :]
    gq_hbm, gk_hbm, gv_hbm, gk_ref, gv_ref, sems = refs
    hbm_of = {"gq": gq_hbm, "gk": gk_hbm, "gv": gv_hbm}
    copies = stores(plan, [s for _, s in finished], done_refs, [hbm_of[name] for name, _ in finished], sems)
    start_all(plan, copies)

    tails = []
    if last_part:
        for n, pair in enumerate(plan.pairs()):
            for m, (ref, target) in enumerate(((gk_ref, gk_hbm), (gv_ref, gv_hbm))):
                start = plan.owner(slot) * plan.span
                width = len(pair) * plan.dim
                lanes = pl.ds(pl.multiple_of(start + n * width, width), width)
                sem = sems.at[len(finished) + 2 * n + m]
                tails.append((slot, pltpu.make_async_copy(ref.at[:, plan.columns(pair)], target.at[:, lanes], sem)))

    @plan.guard(slot)
    def _():
        columns = table_ref[slot].T
        for n, pair in enumerate(plan.pairs()):
            back = diagonal([back_ref[plan.head(i), :] for i in pair])
            both = plan.columns(pair)
            from_values = dot_nt(v_ref[:, both], back)
            from_keys = dot(k_ref[:, both], back)
            for j, i in enumerate(pair):
                lanes, part = plan.head(i), plan.head(j)
                leave = columns[:, 2 * plan.hpo + i : 2 * plan.hpo + i + 1]
                gk_ref[:, lanes] = (gkp_ref[:, lanes] + leave * from_values[:, part]).astype(BF16)
                gv_ref[:, lanes] = (gvp_ref[:, lanes] + leave * from_keys[:, part]).astype(BF16)
            for _, copy in tails[2 * n : 2 * n + 2]:
                copy.start()

    wait_all(plan, copies + tails)


def exchange(arrays, size, halves, target):
    def pairs(slot):
        return [(base + i, base + target(i, slot, size)) for base in range(0, halves * size, size) for i in range(size)]

    return [arrays[0]] + [lax.ppermute(arrays[slot], "seq", pairs(slot)) for slot in range(1, size)]


def per_device(queries, keys, values, cotangent, log_decay, starts):
    length, width = queries.shape
    heads = log_decay.shape[0]
    dim = width // heads
    blocks = lax.axis_size("seq")
    shares = lax.axis_size("head")
    halves = 2 if blocks % 2 == 0 else 1
    size = blocks // halves
    plan = Plan(heads, dim, length, size)
    hpo, span = plan.hpo, plan.span
    params = pltpu.CompilerParams(vmem_limit_bytes=12 << 20)

    inside = pl.BlockSpec(memory_space=pltpu.VMEM)
    unused = pl.BlockSpec(memory_space=pl.ANY)
    hbm = pl.BlockSpec(memory_space=pltpu.HBM)
    dma = pltpu.SemaphoreType.DMA
    whole = pltpu.HBM((length, width), BF16)

    def outside(array):
        return pltpu.with_memory_space_constraint(array, pltpu.HBM)

    def held(dtype, columns=span):
        return pltpu.VMEM((length, columns), dtype)

    def cost(products, exps=0):
        return pl.CostEstimate(flops=2 * hpo * products, bytes_accessed=length * span, transcendentals=hpo * exps)

    def call(kernel, name, operands, results, work, extra=(), scratch=(), aliases=None):
        far = [isinstance(a, tuple) for a in operands]
        return pl.pallas_call(
            kernel,
            in_specs=[hbm if f else inside for f in far] + [unused] * len(extra),
            out_specs=[hbm if r is whole else inside for r in results],
            out_shape=list(results),
            scratch_shapes=list(scratch),
            input_output_aliases=aliases or {},
            compiler_params=params,
            cost_estimate=work,
            name=name,
        )(*[a[0] if f else a for a, f in zip(operands, far)], *extra)

    def scan(arrays, carries, after, later):
        forward = carries is None
        factor = pltpu.VMEM((size, 8, dim), F32)
        local, total, factor, *rest = call(
            functools.partial(scan_kernel, plan, forward),
            "scan",
            [*arrays] + ([] if forward else [carries]),
            [pltpu.VMEM((size, span, dim), F32), pltpu.VMEM((span, dim), BF16), factor] + ([factor] if forward else []),
            None,
            after,
            [pltpu.VMEM((size, *arrays[0].shape), BF16)],
        )
        if halves == 2:
            pairs = [(i, (1 - i // size) * size + mirrored(i % size, 1, size)) for i in range(2 * size)]
            outer = lax.ppermute(total, "seq", pairs)
        else:
            outer = jnp.zeros_like(total)
        back = call(
            functools.partial(return_kernel, plan, forward),
            "return",
            [local, factor, outer],
            [pltpu.VMEM((span, dim), BF16)] * size,
            None,
            later,
        )
        return exchange(back, size, halves, inverse), (rest[0] if forward else None)

    big, small = length * length * dim, length * dim * dim
    queries, keys, values, cotangent = (outside(a) for a in (queries, keys, values, cotangent))
    others = size - 1
    results = call(
        functools.partial(update_kernel, plan),
        "update",
        [(outside(log_decay),), (outside(starts.reshape(1, length)),), (keys,), (values,)],
        [pltpu.VMEM((span + ROWS, dim), BF16)] * others
        + [held(BF16)] * (2 * others)
        + [pltpu.VMEM((span, length), BF16)] * others
        + [pltpu.VMEM((size, ROWS, length), F32)],
        cost(size * small),
        scratch=[
            pltpu.VMEM((heads, length), F32),
            pltpu.VMEM((1, length), jnp.int32),
            pltpu.VMEM((heads // hpo, ROWS, length), F32),
            dma((2,)),
            dma((2, size)),
        ],
    )
    sent, k, v, turned = ([None, *results[i * others : (i + 1) * others]] for i in range(4))
    table = results[-1]
    received = exchange(sent, size, halves, partner)
    own = [held(BF16)] * 2 + [pltpu.VMEM((span, length), BF16), pltpu.VMEM((span + ROWS, dim), BF16)]

    kept = pltpu.VMEM((hpo, length * (length + HALF) // 2 // HALF, HALF), BF16)
    intra, decayed, probs, weights = [], [], [], []
    for slot in range(size):
        first = slot == 0
        results = call(
            functools.partial(intra_kernel, plan, slot, first),
            "intra",
            [table] + ([(a,) for a in (queries, cotangent, keys, values)] if first else [k[slot], v[slot], q[slot], mask]),
            (own + [held(BF16)] * (2 * size) + [pltpu.VMEM((length, length), F32)] if first else [])
            + [held(F32), pltpu.VMEM((span, length), BF16), kept, kept],
            cost(2 * big, length * length),
            scratch=[dma((2 + 2 * size,))] if first else [],
        )
        if first:
            k[0], v[0], turned[0], sent[0], *results = results
            q, cot, mask = results[:size], results[size : 2 * size], results[2 * size]
        for kind, result in zip((intra, decayed, probs, weights), results[-4:]):
            kind.append(result)

    middle = -(-size // 2)
    received[0] = sent[0]
    received, carries = scan(received, None, intra[:middle], intra[middle:])

    outputs = [None] * size
    total = None
    for slot in arrival(size):
        first = slot == 0
        outputs[slot], total = call(
            functools.partial(output_kernel, plan, slot, first),
            "output",
            [table, q[slot], cot[slot], intra[slot], received[slot]] + ([] if first else [total]),
            [held(F32), pltpu.VMEM((2, length, dim), F32)],
            cost(small),
        )
    (sums,) = call(sums_kernel, "sums", [total], [pltpu.VMEM((2 * length // 128, 128), F32)], cost(length))
    states = received

    everyone = [sums] + [
        lax.ppermute(sums, "head", [(i, partner(i, k, shares)) for i in range(shares)]) for k in [*range(2, shares), 1]
    ]

    gout, sent = [None] * size, [None] * size
    factor = None
    for slot in order(size):
        first = factor is None
        *rest, gout[slot], sent[slot] = call(
            functools.partial(gout_kernel, plan, slot, shares if first else 0),
            "gout",
            (everyone if first else [factor]) + [outputs[slot], cot[slot], decayed[slot]],
            ([pltpu.VMEM((2, length, dim), F32)] if first else []) + [held(BF16), pltpu.VMEM((span, dim), BF16)],
            cost(small),
        )
        factor = rest[0] if first else factor
    received = exchange(sent, size, halves, partner)
    attn = call(
        functools.partial(attn_kernel, plan),
        "attn",
        [factor, *outputs],
        [held(BF16)] * size,
        cost(small),
    )

    gq, gk_part, gv_part = [], [], []
    attn_whole = gq_whole = None
    for slot in range(size):
        fresh = slot < 2
        finished = list(range(size)) if slot == 0 else [slot - 1]
        done = list(attn) if slot == 0 else [gq[slot - 1]]
        operands = [table, k[slot], v[slot], q[slot], gout[slot], turned[slot], probs[slot], weights[slot], states[slot]]
        operands += done
        results = call(
            functools.partial(gradient_kernel, plan, slot, finished, fresh),
            "gradient",
            operands + ([] if fresh else [(gq_whole,)]),
            [whole, held(BF16), held(F32), held(F32)],
            cost(4 * big),
            scratch=[dma((len(finished),))],
            aliases={} if fresh else {len(operands): 0},
        )
        if slot == 0:
            attn_whole = results[0]
        else:
            gq_whole = results[0]
        for kind, result in zip((gq, gk_part, gv_part), results[1:]):
            kind.append(result)

    received, _ = scan(received, carries, gk_part[:1], gk_part[1:-1])

    gk_whole = gv_whole = None
    gk = gv = None
    slots = arrival(size)
    for n, slot in enumerate(slots):
        first, last = n == 0, n == size - 1
        finished = [("gq", size - 1)] if first else [("gk", slots[n - 1]), ("gv", slots[n - 1])]
        done = [gq[-1]] if first else [gk, gv]
        operands = [table, k[slot], v[slot], gk_part[slot], gv_part[slot], received[slot]] + done
        held_back = [gq_whole, gk_whole, gv_whole]
        fresh = [a is None for a in held_back]
        aliases = {}
        chained = []
        for m, array in enumerate(held_back):
            if array is not None:
                aliases[len(operands) + len(chained)] = m
                chained.append((array,))
        gq_whole, gk_whole, gv_whole, gk, gv = call(
            functools.partial(final_kernel, plan, slot, finished, fresh, last),
            "final",
            operands + chained,
            [whole] * 3 + [held(BF16)] * 2,
            cost(2 * small),
            scratch=[dma((len(finished) + 2 * len(plan.pairs()),))],
            aliases=aliases,
        )
    return (attn_whole, gq_whole, gk_whole, gv_whole)


def solution(mesh):
    wide = P("seq", "head")
    return jax.shard_map(
        per_device,
        mesh=mesh,
        in_specs=(wide, wide, wide, wide, P("head", "seq"), P("seq")),
        out_specs=(wide, wide, wide, wide),
        check_vma=False,
    )
```

```python
import functools

import jax
import jax.numpy as jnp
from jax import lax
from jax.experimental import pallas as pl
from jax.experimental.pallas import tpu as pltpu
from jax.sharding import PartitionSpec as P

HEAD_TOTAL = 64
HEAD_DIM = 128
EPS = 1e-05
LOG2E = 1.4426950408889634
MASKED = -1e30
ROWS = 16
HALF = 256
F32 = jnp.float32
BF16 = jnp.bfloat16


def dot(a, b, dims=((1,), (0,))):
    return lax.dot_general(a, b, (dims, ((), ())), preferred_element_type=F32)


def dot_nt(a, b):
    return dot(a, b, ((1,), (1,)))


def three_parts(x):
    high = x.astype(BF16).astype(F32)
    rest = x - high
    middle = rest.astype(BF16).astype(F32)
    return high, middle, rest - middle


def lanes_of(index, size):
    return pl.ds(index * size if isinstance(index, int) else pl.multiple_of(index * size, size), size)


def partner(place, slot, size):
    if size & (size - 1):
        return (place + slot) % size
    return place ^ (3 - slot if slot in (1, 2) and size > 2 else slot)


def inverse(place, slot, size):
    return partner(place, slot, size) if size & (size - 1) == 0 else (place + size - slot) % size


def mirrored(place, half, size):
    return place ^ (2 * half) if size == 4 else place


def my_place(size):
    return lax.rem(lax.axis_index("seq"), size)


def ones_where(keep):
    return jnp.where(keep, 1.0, 0.0).astype(BF16)


def running_sum(x, upper):
    rows = x.shape[0]
    parts = jnp.concatenate(three_parts(x), axis=0).astype(BF16)
    sums = dot(parts, upper)
    return sums[:rows] + sums[rows : 2 * rows] + sums[2 * rows :]


def diagonal(blocks):
    if len(blocks) == 1:
        return blocks[0]
    zero = jnp.zeros_like(blocks[0])
    rows = [[block if i == j else zero for j in range(len(blocks))] for i, block in enumerate(blocks)]
    return jnp.concatenate([jnp.concatenate(row, axis=1) for row in rows], axis=0)


def block_mask(table):
    length = table.shape[1]
    row = table[ROWS - 1 :, :]
    column = table.T[:, ROWS - 1 :]
    down = lax.broadcasted_iota(jnp.int32, (length, length), 0)
    across = lax.broadcasted_iota(jnp.int32, (length, length), 1)
    return jnp.where((across >= down) & (row == column), 0.0, MASKED)


class Plan:
    def __init__(self, heads, dim, length, size):
        self.heads, self.dim, self.length, self.size = heads, dim, length, size
        self.hpo = -(-heads // size)
        self.span = self.hpo * dim

    def owner(self, slot):
        return mirrored(partner(my_place(self.size), slot, self.size), lax.axis_index("seq") // self.size, self.size)

    def lanes(self, slot):
        start = self.owner(slot) * self.span
        return pl.ds(pl.multiple_of(start, self.span), self.span)

    def head(self, i):
        return slice(i * self.dim, (i + 1) * self.dim)

    def tiles(self):
        for j in range(self.length // HALF):
            start = HALF * (j * (j + 1) // 2)
            yield slice(j * HALF, (j + 1) * HALF), slice(0, (j + 1) * HALF), slice(start, start + (j + 1) * HALF)

    def pairs(self):
        step = 2 if self.hpo % 2 == 0 else 1
        return [list(range(i, i + step)) for i in range(0, self.hpo, step)]

    def columns(self, pair):
        return slice(pair[0] * self.dim, (pair[-1] + 1) * self.dim)

    def guard(self, slot):
        return pl.when(self.owner(slot) * self.hpo < self.heads)


def order(size):
    return list(range(1, size)) + [0]


def arrival(size):
    return list(range(size))


def update_slot(plan, table, k_ref, v_ref, turned_ref, sent_ref):
    hpo, dim = plan.hpo, plan.dim
    line = lax.broadcasted_iota(jnp.int32, (ROWS, dim), 0)
    tile = jnp.zeros((ROWS, dim), F32)
    for i in range(hpo):
        lanes = plan.head(i)
        turned = k_ref[:, lanes].T
        turned_ref[lanes, :] = turned
        decayed = (turned.astype(F32) * table[2 * hpo + i : 2 * hpo + i + 1]).astype(BF16)
        sent_ref[lanes, :] = dot(decayed, v_ref[:, lanes]).astype(BF16)
        carry = jnp.broadcast_to(table[hpo + i : hpo + i + 1, plan.length - 1 :], (ROWS, dim))
        for j, part in enumerate(three_parts(carry)):
            tile = jnp.where(line == 3 * i + j, part, tile)
    sent_ref[hpo * dim :, :] = tile.astype(BF16)


def update_kernel(plan, logs_hbm, starts_hbm, k_hbm, v_hbm, *refs):
    size, hpo, heads, length = plan.size, plan.hpo, plan.heads, plan.length
    sent_refs, k_refs, v_refs, turned_refs = (refs[i * (size - 1) : (i + 1) * (size - 1)] for i in range(4))
    table_ref, logs_ref, starts_ref, natural_ref, small_sems, sems = refs[4 * (size - 1) :]
    copies = [
        pltpu.make_async_copy(logs_hbm, logs_ref, small_sems.at[0]),
        pltpu.make_async_copy(starts_hbm, starts_ref, small_sems.at[1]),
    ]
    for copy in copies:
        copy.start()

    def loads(slot):
        lanes = plan.lanes(slot)
        return (
            pltpu.make_async_copy(k_hbm.at[:, lanes], k_refs[slot - 1], sems.at[0, slot]),
            pltpu.make_async_copy(v_hbm.at[:, lanes], v_refs[slot - 1], sems.at[1, slot]),
        )

    for slot in range(1, size):

        @plan.guard(slot)
        def _():
            for copy in loads(slot):
                copy.start()

    down = lax.broadcasted_iota(jnp.int32, (length, length), 0)
    across = lax.broadcasted_iota(jnp.int32, (length, length), 1)
    upper = ones_where(down <= across)
    for copy in copies:
        copy.wait()
    flags = jnp.broadcast_to(starts_ref[...].astype(F32), (8, length))
    sums = running_sum(jnp.concatenate([logs_ref[...], flags], axis=0), upper)
    logs, count = sums[:heads] * LOG2E, sums[heads : heads + 1]
    last = slice(length - 1, length)
    enter = jnp.where(count == 0.0, jnp.exp2(logs), 0.0)
    leave = jnp.where(count == count[:, last], jnp.exp2(logs[:, last] - logs), 0.0)
    fill = jnp.broadcast_to(count, (ROWS - 3 * hpo, length))
    for owner in range(heads // hpo):
        rows = slice(owner * hpo, (owner + 1) * hpo)
        natural_ref[owner] = jnp.concatenate([logs[rows], enter[rows], leave[rows], fill], axis=0)
    table_ref[0] = natural_ref[jnp.minimum(plan.owner(0), heads // hpo - 1)]

    for slot in range(1, size):

        @plan.guard(slot)
        def _():
            table = natural_ref[plan.owner(slot)]
            table_ref[slot] = table
            for copy in loads(slot):
                copy.wait()
            n = slot - 1
            update_slot(plan, table, k_refs[n], v_refs[n], turned_refs[n], sent_refs[n])


def scan_kernel(plan, forward, *refs):
    size, hpo, dim = plan.size, plan.hpo, plan.dim
    in_refs, refs = refs[:size], refs[size:]
    if forward:
        local_ref, total_ref, factor_ref, carry_ref, ordered_ref = refs[-5:]
    else:
        carry_ref = refs[0]
        local_ref, total_ref, factor_ref, ordered_ref = refs[-4:]
    me = my_place(size)
    for slot, in_ref in enumerate(in_refs):
        ordered_ref[inverse(me, slot, size)] = in_ref[...]
    if forward:
        for b in range(size):
            tile = ordered_ref[b, hpo * dim :, :].astype(F32)
            for i in range(hpo):
                carry_ref[b, i : i + 1, :] = tile[3 * i : 3 * i + 1] + tile[3 * i + 1 : 3 * i + 2] + tile[3 * i + 2 : 3 * i + 3]
    for i in range(hpo):
        rows = plan.head(i)
        state = jnp.zeros((dim, dim), F32)
        factor = jnp.ones((1, dim), F32)
        for b in range(size) if forward else reversed(range(size)):
            carry = carry_ref[b, i : i + 1, :]
            local_ref[b, rows, :] = state
            factor_ref[b, i : i + 1, :] = factor
            state = carry * state + ordered_ref[b, rows, :].astype(F32)
            factor = factor * carry
        total_ref[rows, :] = state.astype(BF16)


def return_kernel(plan, forward, local_ref, factor_ref, outer_ref, *refs):
    out_refs = refs[-plan.size :]
    me = my_place(plan.size)
    upper = lax.axis_index("seq") >= plan.size
    takes = upper if forward else jnp.logical_not(upper)
    for i in range(plan.hpo):
        rows = plan.head(i)
        outer = jnp.where(takes, outer_ref[rows, :].astype(F32), 0.0)
        for slot, out_ref in enumerate(out_refs):
            b = inverse(me, slot, plan.size)
            out_ref[rows, :] = (local_ref[b, rows, :] + factor_ref[b, i : i + 1, :] * outer).astype(BF16)


def intra_kernel(plan, slot, first_part, table_ref, *refs):
    size, hpo, length = plan.size, plan.hpo, plan.length
    copies = []
    if first_part:
        q_hbm, cot_hbm, k_hbm, v_hbm, k_ref, v_ref, turned_ref, sent_ref = refs[:8]
        q_refs, cot_refs = refs[8 : 8 + size], refs[8 + size : 8 + 2 * size]
        mask_ref, out_ref, decayed_ref, probs_ref, weight_ref, sems = refs[8 + 2 * size :]
        q_ref = q_refs[slot]
        first = [(slot, k_hbm, k_ref), (slot, v_hbm, v_ref), (slot, q_hbm, q_ref)]
        rest = [(other, q_hbm, q_refs[other]) for other in range(size) if other != slot]
        rest += [(other, cot_hbm, cot_refs[other]) for other in range(size)]
        copies = [
            (other, pltpu.make_async_copy(source.at[:, plan.lanes(other)], target, sems.at[n]))
            for n, (other, source, target) in enumerate(first + rest)
        ]
        start_all(plan, copies)
        mask_ref[...] = block_mask(table_ref[0])
        wait_all(plan, copies[:2])
    else:
        k_ref, v_ref, q_ref, mask_ref, out_ref, decayed_ref, probs_ref, weight_ref = refs

    @plan.guard(slot)
    def _():
        table = table_ref[slot]
        columns = table.T
        if first_part:
            update_slot(plan, table, k_ref, v_ref, turned_ref, sent_ref)
            copies[2][1].wait()
        for i in range(hpo):
            lanes = plan.head(i)
            turned = q_ref[:, lanes].T
            decayed_ref[lanes, :] = (turned.astype(F32) * table[hpo + i : hpo + i + 1]).astype(BF16)
            for later, seen, kept in plan.tiles():
                gap = table[i : i + 1, later] - columns[seen, i : i + 1]
                weight = jnp.exp2(gap + mask_ref[seen, later])
                probs = (dot(k_ref[seen, lanes], turned[:, later]) * weight).astype(BF16)
                weight_ref[i, kept, :] = weight.astype(BF16)
                probs_ref[i, kept, :] = probs
                out_ref[later, lanes] = dot(probs, v_ref[seen, lanes], ((0,), (0,)))

    wait_all(plan, copies[3:])


def token_rows(total):
    rows = [jnp.sum(total[i : i + 128].T, axis=0, keepdims=True) for i in range(0, total.shape[0], 128)]
    return jnp.concatenate(rows, axis=0)


def sums_kernel(total_ref, sums_ref):
    sums_ref[...] = jnp.concatenate([token_rows(total_ref[0]), token_rows(total_ref[1])], axis=0)


def output_kernel(plan, slot, first_part, table_ref, q_ref, cot_ref, intra_ref, state_ref, *refs):
    hpo = plan.hpo
    if not first_part:
        old_ref, refs = refs[0], refs[1:]
    out_ref, total_ref = refs[:2]
    if first_part:
        total_ref[...] = jnp.zeros_like(total_ref)
    else:
        total_ref[...] = old_ref[...]

    @plan.guard(slot)
    def _():
        columns = table_ref[slot].T
        square, cross = total_ref[0], total_ref[1]
        for pair in plan.pairs():
            states = diagonal([state_ref[plan.head(i), :] for i in pair])
            both = dot(q_ref[:, plan.columns(pair)], states)
            for j, i in enumerate(pair):
                lanes = plan.head(i)
                out = intra_ref[:, lanes] + columns[:, hpo + i : hpo + i + 1] * both[:, plan.head(j)]
                out_ref[:, lanes] = out
                square = square + out * out
                cross = cross + cot_ref[:, lanes].astype(F32) * out
        total_ref[0] = square
        total_ref[1] = cross


def factors(sums_refs, factor_ref):
    total = sums_refs[0][...]
    for ref in sums_refs[1:]:
        total = total + ref[...]
    lines = total.shape[0] // 2
    full = HEAD_TOTAL * HEAD_DIM
    scale = lax.rsqrt(total[:lines] / full + EPS)
    slope = scale * scale * scale * total[lines:] / full
    turned = jnp.concatenate([scale, slope], axis=0).T
    for j in range(2):
        for i in range(lines):
            column = turned[:, j * lines + i : j * lines + i + 1]
            factor_ref[j, i * 128 : (i + 1) * 128, :] = jnp.broadcast_to(column, (128, factor_ref.shape[2]))


def gout_kernel(plan, slot, count, *refs):
    if count:
        factor_ref = refs[count + 3]
        factors(refs[:count], factor_ref)
        out_ref, cot_ref, decayed_ref, _, gout_ref, sent_ref = refs[count:]
    else:
        factor_ref, out_ref, cot_ref, decayed_ref, gout_ref, sent_ref = refs

    @plan.guard(slot)
    def _():
        for i in range(plan.hpo):
            lanes = plan.head(i)
            gout = factor_ref[0] * cot_ref[:, lanes].astype(F32) - factor_ref[1] * out_ref[:, lanes]
            gout = gout.astype(BF16)
            gout_ref[:, lanes] = gout
            sent_ref[lanes, :] = dot(decayed_ref[lanes, :], gout).astype(BF16)


def attn_kernel(plan, factor_ref, *refs):
    size = plan.size
    for slot, (out_ref, attn_ref) in enumerate(zip(refs[:size], refs[size:])):

        @plan.guard(slot)
        def _():
            for i in range(plan.hpo):
                lanes = plan.head(i)
                attn_ref[:, lanes] = (factor_ref[0] * out_ref[:, lanes]).astype(BF16)


def stores(plan, slots, in_refs, hbms, sems):
    return [
        (slot, pltpu.make_async_copy(ref, hbm.at[:, plan.lanes(slot)], sems.at[n]))
        for n, (slot, ref, hbm) in enumerate(zip(slots, in_refs, hbms))
    ]


def start_all(plan, copies):
    for slot, copy in copies:
        plan.guard(slot)(copy.start)


def wait_all(plan, copies):
    for slot, copy in copies:
        plan.guard(slot)(copy.wait)


def gradient_kernel(plan, slot, finished, fresh, *refs):
    table_ref, k_ref, v_ref, q_ref, gout_ref, turned_ref, probs_ref, weight_ref, state_ref = refs[:9]
    refs = refs[9:]
    done_refs, refs = refs[: len(finished)], refs[len(finished) :]
    copies = []
    if finished:
        if not fresh:
            refs = refs[1:]
        copies = stores(plan, finished, done_refs, [refs[0]] * len(finished), refs[-1])
        refs = refs[1:-1]
    start_all(plan, copies)
    gq_ref, gk_ref, gv_ref = refs
    hpo, length = plan.hpo, plan.length

    @plan.guard(slot)
    def _():
        table = table_ref[slot]
        for i in range(hpo):
            lanes = plan.head(i)
            gout_turned = gout_ref[:, lanes].T
            carried = table[hpo + i : hpo + i + 1] * dot(state_ref[lanes, :], gout_turned)
            tiles = list(plan.tiles())
            grads = [None] * len(tiles)
            for j, (later, seen, kept) in reversed(list(enumerate(tiles))):
                product = dot(v_ref[seen, lanes], gout_turned[:, later])
                grads[j] = (product * weight_ref[i, kept, :].astype(F32)).astype(BF16)
            probs = [probs_ref[i, kept, :] for _, _, kept in tiles]
            for target, lefts, right_ref in ((gv_ref, probs, gout_ref), (gk_ref, grads, q_ref)):
                parts = [dot(left, right_ref[later, lanes]) for left, (later, _, _) in zip(lefts, tiles)]
                for j, (rows, _, _) in enumerate(tiles):
                    target[rows, lanes] = functools.reduce(jnp.add, [part[rows] for part in reversed(parts[j:])])
            for grad, (later, seen, _) in zip(grads, tiles):
                total = carried[:, later] + dot(turned_ref[lanes, seen], grad)
                gq_ref[later, lanes] = total.astype(BF16).T

    wait_all(plan, copies)


def final_kernel(plan, slot, finished, fresh, last_part, *refs):
    table_ref, k_ref, v_ref, gkp_ref, gvp_ref, back_ref = refs[:6]
    refs = refs[6:]
    done_refs, refs = refs[: len(finished)], refs[len(finished) :]
    if not all(fresh):
        refs = refs[fresh.count(False) :]
    gq_hbm, gk_hbm, gv_hbm, gk_ref, gv_ref, sems = refs
    hbm_of = {"gq": gq_hbm, "gk": gk_hbm, "gv": gv_hbm}
    copies = stores(plan, [s for _, s in finished], done_refs, [hbm_of[name] for name, _ in finished], sems)
    start_all(plan, copies)

    tails = []
    if last_part:
        for n, pair in enumerate(plan.pairs()):
            for m, (ref, target) in enumerate(((gk_ref, gk_hbm), (gv_ref, gv_hbm))):
                start = plan.owner(slot) * plan.span
                width = len(pair) * plan.dim
                lanes = pl.ds(pl.multiple_of(start + n * width, width), width)
                sem = sems.at[len(finished) + 2 * n + m]
                tails.append((slot, pltpu.make_async_copy(ref.at[:, plan.columns(pair)], target.at[:, lanes], sem)))

    @plan.guard(slot)
    def _():
        columns = table_ref[slot].T
        for n, pair in enumerate(plan.pairs()):
            back = diagonal([back_ref[plan.head(i), :] for i in pair])
            both = plan.columns(pair)
            from_values = dot_nt(v_ref[:, both], back)
            from_keys = dot(k_ref[:, both], back)
            for j, i in enumerate(pair):
                lanes, part = plan.head(i), plan.head(j)
                leave = columns[:, 2 * plan.hpo + i : 2 * plan.hpo + i + 1]
                gk_ref[:, lanes] = (gkp_ref[:, lanes] + leave * from_values[:, part]).astype(BF16)
                gv_ref[:, lanes] = (gvp_ref[:, lanes] + leave * from_keys[:, part]).astype(BF16)
            for _, copy in tails[2 * n : 2 * n + 2]:
                copy.start()

    wait_all(plan, copies + tails)


def exchange(arrays, size, halves, target):
    def pairs(slot):
        return [(base + i, base + target(i, slot, size)) for base in range(0, halves * size, size) for i in range(size)]

    return [arrays[0]] + [lax.ppermute(arrays[slot], "seq", pairs(slot)) for slot in range(1, size)]


def per_device(queries, keys, values, cotangent, log_decay, starts):
    length, width = queries.shape
    heads = log_decay.shape[0]
    dim = width // heads
    blocks = lax.axis_size("seq")
    shares = lax.axis_size("head")
    halves = 2 if blocks % 2 == 0 else 1
    size = blocks // halves
    plan = Plan(heads, dim, length, size)
    hpo, span = plan.hpo, plan.span
    params = pltpu.CompilerParams(vmem_limit_bytes=12 << 20)

    inside = pl.BlockSpec(memory_space=pltpu.VMEM)
    unused = pl.BlockSpec(memory_space=pl.ANY)
    hbm = pl.BlockSpec(memory_space=pltpu.HBM)
    dma = pltpu.SemaphoreType.DMA
    whole = pltpu.HBM((length, width), BF16)

    def outside(array):
        return pltpu.with_memory_space_constraint(array, pltpu.HBM)

    def held(dtype, columns=span):
        return pltpu.VMEM((length, columns), dtype)

    def cost(products, exps=0):
        return pl.CostEstimate(flops=2 * hpo * products, bytes_accessed=length * span, transcendentals=hpo * exps)

    def call(kernel, name, operands, results, work, extra=(), scratch=(), aliases=None):
        far = [isinstance(a, tuple) for a in operands]
        return pl.pallas_call(
            kernel,
            in_specs=[hbm if f else inside for f in far] + [unused] * len(extra),
            out_specs=[hbm if r is whole else inside for r in results],
            out_shape=list(results),
            scratch_shapes=list(scratch),
            input_output_aliases=aliases or {},
            compiler_params=params,
            cost_estimate=work,
            name=name,
        )(*[a[0] if f else a for a, f in zip(operands, far)], *extra)

    def scan(arrays, carries, after, later):
        forward = carries is None
        factor = pltpu.VMEM((size, 8, dim), F32)
        local, total, factor, *rest = call(
            functools.partial(scan_kernel, plan, forward),
            "scan",
            [*arrays] + ([] if forward else [carries]),
            [pltpu.VMEM((size, span, dim), F32), pltpu.VMEM((span, dim), BF16), factor] + ([factor] if forward else []),
            None,
            after,
            [pltpu.VMEM((size, *arrays[0].shape), BF16)],
        )
        if halves == 2:
            pairs = [(i, (1 - i // size) * size + mirrored(i % size, 1, size)) for i in range(2 * size)]
            outer = lax.ppermute(total, "seq", pairs)
        else:
            outer = jnp.zeros_like(total)
        back = call(
            functools.partial(return_kernel, plan, forward),
            "return",
            [local, factor, outer],
            [pltpu.VMEM((span, dim), BF16)] * size,
            None,
            later,
        )
        return exchange(back, size, halves, inverse), (rest[0] if forward else None)

    big, small = length * length * dim, length * dim * dim
    queries, keys, values, cotangent = (outside(a) for a in (queries, keys, values, cotangent))
    others = size - 1
    results = call(
        functools.partial(update_kernel, plan),
        "update",
        [(outside(log_decay),), (outside(starts.reshape(1, length)),), (keys,), (values,)],
        [pltpu.VMEM((span + ROWS, dim), BF16)] * others
        + [held(BF16)] * (2 * others)
        + [pltpu.VMEM((span, length), BF16)] * others
        + [pltpu.VMEM((size, ROWS, length), F32)],
        cost(size * small),
        scratch=[
            pltpu.VMEM((heads, length), F32),
            pltpu.VMEM((1, length), jnp.int32),
            pltpu.VMEM((heads // hpo, ROWS, length), F32),
            dma((2,)),
            dma((2, size)),
        ],
    )
    sent, k, v, turned = ([None, *results[i * others : (i + 1) * others]] for i in range(4))
    table = results[-1]
    received = exchange(sent, size, halves, partner)
    own = [held(BF16)] * 2 + [pltpu.VMEM((span, length), BF16), pltpu.VMEM((span + ROWS, dim), BF16)]

    kept = pltpu.VMEM((hpo, length * (length + HALF) // 2 // HALF, HALF), BF16)
    intra, decayed, probs, weights = [], [], [], []
    for slot in range(size):
        first = slot == 0
        results = call(
            functools.partial(intra_kernel, plan, slot, first),
            "intra",
            [table] + ([(a,) for a in (queries, cotangent, keys, values)] if first else [k[slot], v[slot], q[slot], mask]),
            (own + [held(BF16)] * (2 * size) + [pltpu.VMEM((length, length), F32)] if first else [])
            + [held(F32), pltpu.VMEM((span, length), BF16), kept, kept],
            cost(2 * big, length * length),
            scratch=[dma((2 + 2 * size,))] if first else [],
        )
        if first:
            k[0], v[0], turned[0], sent[0], *results = results
            q, cot, mask = results[:size], results[size : 2 * size], results[2 * size]
        for kind, result in zip((intra, decayed, probs, weights), results[-4:]):
            kind.append(result)

    middle = -(-size // 2)
    received[0] = sent[0]
    received, carries = scan(received, None, intra[:middle], intra[middle:])

    outputs = [None] * size
    total = None
    for slot in arrival(size):
        first = slot == 0
        outputs[slot], total = call(
            functools.partial(output_kernel, plan, slot, first),
            "output",
            [table, q[slot], cot[slot], intra[slot], received[slot]] + ([] if first else [total]),
            [held(F32), pltpu.VMEM((2, length, dim), F32)],
            cost(small),
        )
    (sums,) = call(sums_kernel, "sums", [total], [pltpu.VMEM((2 * length // 128, 128), F32)], cost(length))
    states = received

    everyone = [sums] + [
        lax.ppermute(sums, "head", [(i, partner(i, k, shares)) for i in range(shares)]) for k in [*range(2, shares), 1]
    ]

    gout, sent = [None] * size, [None] * size
    factor = None
    for slot in order(size):
        first = factor is None
        *rest, gout[slot], sent[slot] = call(
            functools.partial(gout_kernel, plan, slot, shares if first else 0),
            "gout",
            (everyone if first else [factor]) + [outputs[slot], cot[slot], decayed[slot]],
            ([pltpu.VMEM((2, length, dim), F32)] if first else []) + [held(BF16), pltpu.VMEM((span, dim), BF16)],
            cost(small),
        )
        factor = rest[0] if first else factor
    received = exchange(sent, size, halves, partner)
    attn = call(
        functools.partial(attn_kernel, plan),
        "attn",
        [factor, *outputs],
        [held(BF16)] * size,
        cost(small),
    )

    gq, gk_part, gv_part = [], [], []
    attn_whole = gq_whole = None
    for slot in range(size):
        fresh = slot < 2
        finished = list(range(size)) if slot == 0 else [slot - 1]
        done = list(attn) if slot == 0 else [gq[slot - 1]]
        operands = [table, k[slot], v[slot], q[slot], gout[slot], turned[slot], probs[slot], weights[slot], states[slot]]
        operands += done
        results = call(
            functools.partial(gradient_kernel, plan, slot, finished, fresh),
            "gradient",
            operands + ([] if fresh else [(gq_whole,)]),
            [whole, held(BF16), held(F32), held(F32)],
            cost(4 * big),
            scratch=[dma((len(finished),))],
            aliases={} if fresh else {len(operands): 0},
        )
        if slot == 0:
            attn_whole = results[0]
        else:
            gq_whole = results[0]
        for kind, result in zip((gq, gk_part, gv_part), results[1:]):
            kind.append(result)

    received, _ = scan(received, carries, gk_part[:1], gk_part[1:-1])

    gk_whole = gv_whole = None
    gk = gv = None
    slots = arrival(size)
    for n, slot in enumerate(slots):
        first, last = n == 0, n == size - 1
        finished = [("gq", size - 1)] if first else [("gk", slots[n - 1]), ("gv", slots[n - 1])]
        done = [gq[-1]] if first else [gk, gv]
        operands = [table, k[slot], v[slot], gk_part[slot], gv_part[slot], received[slot]] + done
        held_back = [gq_whole, gk_whole, gv_whole]
        fresh = [a is None for a in held_back]
        aliases = {}
        chained = []
        for m, array in enumerate(held_back):
            if array is not None:
                aliases[len(operands) + len(chained)] = m
                chained.append((array,))
        gq_whole, gk_whole, gv_whole, gk, gv = call(
            functools.partial(final_kernel, plan, slot, finished, fresh, last),
            "final",
            operands + chained,
            [whole] * 3 + [held(BF16)] * 2,
            cost(2 * small),
            scratch=[dma((len(finished) + 2 * len(plan.pairs()),))],
            aliases=aliases,
        )
    return (attn_whole, gq_whole, gk_whole, gv_whole)


def solution(mesh):
    wide = P("seq", "head")
    return jax.shard_map(
        per_device,
        mesh=mesh,
        in_specs=(wide, wide, wide, wide, P("head", "seq"), P("seq")),
        out_specs=(wide, wide, wide, wide),
        check_vma=False,
    )
```
